32 devices in a mesh: gx: 4 (over x, core), gy: 8 (over z, y).
Axes of the slice: x: 2, y: 2, z: 4, core: 2. Of those that a mesh axis runs over, the one named last changes fastest.
Arguments:
- solution: float32 [32, 64, 512], P('gx', 'gy'), may hold values from -6 to 6
- right_side: float32 [32, 64, 512], P('gx', 'gy'), may hold values from -6 to 6
- alpha: bfloat16 [32, 64, 512], P('gx', 'gy'), may hold values from 0.5 to 2
- beta_x: bfloat16 [32, 64, 512], P('gx', 'gy'), may hold values from 0.25 to 2.5
- beta_y: bfloat16 [32, 64, 512], P('gx', 'gy'), may hold values from 0.25 to 2.5
- beta_z: bfloat16 [32, 64, 512], P('gx', 'gy'), may hold values from 0.25 to 2.5
Outputs:
- fine_iterate: float32 [32, 64, 512], P('gx', 'gy')
- middle_iterate: float32 [16, 32, 256], P('gx', 'gy')
- coarse_iterate: float32 [8, 16, 128], P('gx', 'gy')
The draws below stay inside these ranges and needn't reach their ends.
All inputs are finite; a program needn't handle non-finite values.
Results may differ from the reference program's by a relative error of at most 0.0003.
Values sent between devices are 32-bit elements; how exact they have to be, the bound alone decides.
A program may use at most 64 MiB of HBM per device.

```python
import math
import jax
import jax.numpy as jnp
from jax import lax

LEVELS = 3
SWEEPS = 2
NX = 32
NY = 64
NZ = 512


def shard_levels(own_key, dims, pieces, least, top_value):
    factor_of, own = 1.0, jax.random.fold_in(own_key, 6)
    for dim, blocks in pieces:
        draws = jnp.exp(jax.random.uniform(jax.random.fold_in(own, dim), (blocks,), jnp.float32, least / len(pieces), top_value / len(pieces)))
        factor_of = factor_of * jnp.repeat(draws, dims[dim] // blocks).reshape([-1 if axis == dim else 1 for axis in range(len(dims))])
    return factor_of


def bell_draw(stream_key, dims, deviation, reach, split=(), held_as=jnp.bfloat16):
    entries = jax.random.normal(stream_key, dims, jnp.float32) * deviation
    if len(split) > 0:
        entries = shard_levels(stream_key, dims, split, -0.22, 0.18) * entries
    return jnp.clip(entries, min=-reach, max=reach).astype(held_as)


def setup_inputs(seed: int = 0) -> dict:
    key_of = jax.random.split(jax.random.key(seed), 7)
    return {
        "solution": bell_draw(key_of[0], (NX, NY, NZ), 1.0, 6.0, ((0, 4), (1, 8)), jnp.float32),
        "right_side": bell_draw(key_of[1], (NX, NY, NZ), 1.0, 6.0, ((0, 4), (1, 8)), jnp.float32),
        "alpha": jnp.clip(0.5 + 1.5 * jax.random.uniform(key_of[2], (NX, NY, NZ), jnp.float32) ** shard_levels(key_of[2], (NX, NY, NZ), ((0, 4), (1, 8)), -0.2, 0.2), 0.5, 2.0).astype(jnp.bfloat16),
        "beta_x": jnp.clip(jnp.exp(math.log(2.5) - 2.3025851 * jax.random.uniform(key_of[3], (NX, NY, NZ), jnp.float32) ** shard_levels(key_of[3], (NX, NY, NZ), ((0, 4), (1, 8)), -0.2, 0.2)), 0.25, 2.5).astype(jnp.bfloat16),
        "beta_y": jnp.clip(jnp.exp(math.log(2.5) - 2.3025851 * jax.random.uniform(key_of[4], (NX, NY, NZ), jnp.float32) ** shard_levels(key_of[4], (NX, NY, NZ), ((0, 4), (1, 8)), -0.2, 0.2)), 0.25, 2.5).astype(jnp.bfloat16),
        "beta_z": jnp.clip(jnp.exp(math.log(2.5) - 2.3025851 * jax.random.uniform(key_of[5], (NX, NY, NZ), jnp.float32) ** shard_levels(key_of[5], (NX, NY, NZ), ((0, 4), (1, 8)), -0.2, 0.2)), 0.25, 2.5).astype(jnp.bfloat16),
    }


def shift_up(field, axis):
    size = field.shape[axis]
    rest = lax.slice_in_dim(field, 1, size, axis=axis)
    edge = jnp.zeros_like(lax.slice_in_dim(field, 0, 1, axis=axis))
    return jnp.concatenate([rest, edge], axis=axis)


def shift_down(field, axis):
    size = field.shape[axis]
    rest = lax.slice_in_dim(field, 0, size - 1, axis=axis)
    edge = jnp.zeros_like(lax.slice_in_dim(field, 0, 1, axis=axis))
    return jnp.concatenate([edge, rest], axis=axis)


def stencil(field, beside, coefs, scale):
    out = coefs[0] * field
    for direc in range(3):
        upper_face = coefs[1 + 2 * direc]
        lower_face = coefs[2 + 2 * direc]
        out = out + scale * (upper_face * (field - beside[2 * direc]) + lower_face * (field - beside[2 * direc + 1]))
    return out


def diagonal_of(coefs, scale):
    return coefs[0] + scale * ((coefs[1] + coefs[2]) + (coefs[3] + coefs[4]) + (coefs[5] + coefs[6]))


def parity_of(shape):
    total = lax.broadcasted_iota(jnp.int32, shape, 0) + lax.broadcasted_iota(jnp.int32, shape, 1) + lax.broadcasted_iota(jnp.int32, shape, 2)
    return total % 2


def all_beside(field):
    return (shift_up(field, 0), shift_down(field, 0), shift_up(field, 1), shift_down(field, 1), shift_up(field, 2), shift_down(field, 2))


def coarsen_cells(field):
    nx, ny, nz = field.shape
    return field.reshape(nx // 2, 2, ny // 2, 2, nz // 2, 2).mean(axis=(1, 3, 5))


def coarsen_faces(bx, by, bz):
    nx, ny, nz = bx.shape
    cx = bx[1::2].reshape(nx // 2, ny // 2, 2, nz // 2, 2).mean(axis=(2, 4))
    cy = by[:, 1::2].reshape(nx // 2, 2, ny // 2, nz // 2, 2).mean(axis=(1, 4))
    cz = bz[:, :, 1::2].reshape(nx // 2, 2, ny // 2, 2, nz // 2).mean(axis=(1, 3))
    return cx, cy, cz


def reference(solution, right_side, alpha, beta_x, beta_y, beta_z):
    iterate = solution
    source = right_side
    cell_coef = alpha.astype(jnp.float32)
    face_x = beta_x.astype(jnp.float32)
    face_y = beta_y.astype(jnp.float32)
    face_z = beta_z.astype(jnp.float32)
    results = []
    for level in range(LEVELS):
        scale = 0.25 ** level
        coefs = (cell_coef, face_x, shift_down(face_x, 0), face_y, shift_down(face_y, 1), face_z, shift_down(face_z, 2))
        diag = diagonal_of(coefs, scale)
        parity = parity_of(iterate.shape)
        for sweep in range(SWEEPS):
            for colour in (0, 1):
                resid = source - stencil(iterate, all_beside(iterate), coefs, scale)
                iterate = jnp.where(parity == colour, iterate + resid / diag, iterate)
        results.append(iterate)
        if level + 1 < LEVELS:
            resid = source - stencil(iterate, all_beside(iterate), coefs, scale)
            source = coarsen_cells(resid)
            cell_coef = coarsen_cells(cell_coef)
            face_x, face_y, face_z = coarsen_faces(face_x, face_y, face_z)
            iterate = jnp.zeros_like(source)
    return (results[0], results[1], results[2])
```

```python
import functools

import jax
import jax.numpy as jnp
from jax import lax
from jax.experimental import pallas as pl
from jax.experimental.pallas import tpu as pltpu
from jax.sharding import PartitionSpec as P

LEVELS = 3
ROW = 8

FACES = ((1, 0), (-1, 0), (0, 1), (0, -1))
CORNERS = ((1, 1), (1, -1), (-1, 1), (-1, -1))
AROUND = FACES + CORNERS


def layer_shape(dims, way):
    nx, ny, nz = dims
    return (1 if way[0] else nx, 1 if way[1] else ny, nz)


def edge_shape(dims, way):
    return (2, 1, 1, dims[2])


def messages(dims_of):
    found = {}
    for way in FACES:
        found[("first", 0, way)] = layer_shape(dims_of[0], way)
    for level, dims in enumerate(dims_of):
        for way in ((1, 0), (0, 1)):
            found[("lower", level, way)] = layer_shape(dims, way)
        for way in FACES:
            found[("toward", level, way)] = layer_shape(dims, way)
            found[("ends", level, way)] = edge_shape(dims, way)
        for half in range(2):
            ways = FACES if (level == LEVELS - 1 and half == 1) else AROUND
            for way in ways:
                found[("half%d" % half, level, way)] = layer_shape(dims, way)
    return found


def at_side(dims, way):
    nx, ny, _ = dims
    xs = {0: slice(0, nx), 1: slice(nx - 1, nx), -1: slice(0, 1)}[way[0]]
    ys = {0: slice(0, ny), 1: slice(ny - 1, ny), -1: slice(0, 1)}[way[1]]
    return xs, ys


def halo_place(dims, way):
    nx, ny, _ = dims
    xs = {0: slice(1, 1 + nx), 1: slice(nx + 1, nx + 2), -1: slice(0, 1)}[way[0]]
    ys = {0: slice(ROW, ROW + ny), 1: slice(ROW + ny, ROW + ny + 1), -1: slice(ROW - 1, ROW)}[way[1]]
    return xs, ys


def parity_at(shape, offset=0):
    total = (
        lax.broadcasted_iota(jnp.int32, shape, 0)
        + lax.broadcasted_iota(jnp.int32, shape, 1)
        + lax.broadcasted_iota(jnp.int32, shape, 2)
        + offset
    )
    return (total & 1) == 1


def kernel(dims_of, keys, *refs):
    refs = list(refs)
    u_in, f_in, a_in, bx_in, by_in, bz_in = refs[:6]
    outs = refs[6:9]
    refs = refs[9:]
    n_keys = len(keys)
    out_buf = dict(zip(keys, refs[:n_keys]))
    in_buf = dict(zip(keys, refs[n_keys : 2 * n_keys]))
    refs = refs[2 * n_keys :]
    names = ("open", "shut", "g", "diag", "xu", "xl", "yu", "yl", "zu", "zl", "a", "bx", "by", "bz")
    per = []
    for level in range(LEVELS):
        per.append(dict(zip(names, refs[: len(names)])))
        refs = refs[len(names) :]
    pair_t, cols_t = refs[0:2], refs[2:4]
    send_sem, recv_sem = refs[4], refs[5]

    gx, gy = lax.axis_index("gx"), lax.axis_index("gy")
    n_x, n_y = lax.axis_size("gx"), lax.axis_size("gy")

    def inside(dx, dy):
        ok = None
        for place, step, count in ((gx, dx, n_x), (gy, dy, n_y)):
            if step == 0:
                continue
            here = (place + step < count) if step > 0 else (place + step >= 0)
            ok = here if ok is None else jnp.logical_and(ok, here)
        return ok

    def copy_of(key):
        way = key[2]
        index = keys.index(key)
        return pltpu.make_async_remote_copy(
            src_ref=out_buf[key],
            dst_ref=in_buf[key],
            send_sem=send_sem.at[index],
            recv_sem=recv_sem.at[index],
            device_id={"gx": gx + way[0], "gy": gy + way[1]},
            device_id_type=pl.DeviceIdType.MESH,
        )

    def send(group):
        for way in AROUND:
            chosen = [key for key in group if key[2] == way]
            if chosen:

                @pl.when(inside(*way))
                def _():
                    for key in chosen:
                        copy_of(key).start()

    def receive(group):
        for way in AROUND:
            chosen = [key for key in group if key[2] == way]
            if chosen:

                @pl.when(inside(-way[0], -way[1]))
                def _():
                    for key in chosen:
                        copy_of(key).wait_recv()

    def group_of(kind, level):
        return [key for key in keys if key[0] == kind and key[1] == level]

    barrier = pltpu.get_barrier_semaphore()
    for way in AROUND:

        @pl.when(inside(*way))
        def _():
            pl.semaphore_signal(
                barrier,
                inc=1,
                device_id={"gx": gx + way[0], "gy": gy + way[1]},
                device_id_type=pl.DeviceIdType.MESH,
            )

    per[0]["a"][...] = a_in[...].astype(jnp.float32)
    per[0]["bx"][...] = bx_in[...].astype(jnp.float32)
    per[0]["by"][...] = by_in[...].astype(jnp.float32)
    per[0]["bz"][...] = bz_in[...].astype(jnp.float32)

    def put_faces(kind, level, source, ways):
        for way in ways:
            xs, ys = at_side(dims_of[level], way)
            out_buf[(kind, level, way)][...] = source[xs, ys, :]

    put_faces("first", 0, u_in, FACES)

    def put_lower(level):
        for way, name in (((1, 0), "bx"), ((0, 1), "by")):
            xs, ys = at_side(dims_of[level], way)
            out_buf[("lower", level, way)][...] = per[level][name][xs, ys, :]

    put_lower(0)

    for way in AROUND:
        chosen = [key for key in keys if key[2] == way]

        @pl.when(jnp.logical_not(inside(-way[0], -way[1])))
        def _():
            for key in chosen:
                in_buf[key][...] = jnp.zeros(in_buf[key].shape, jnp.float32)

    beside_x = (gx > 0).astype(jnp.int32) + (gx + 1 < n_x).astype(jnp.int32)
    beside_y = (gy > 0).astype(jnp.int32) + (gy + 1 < n_y).astype(jnp.int32)
    pl.semaphore_wait(barrier, beside_x + beside_y + beside_x * beside_y)

    send(group_of("first", 0) + group_of("lower", 0))

    def pair_matrix(size):
        fine = lax.broadcasted_iota(jnp.int32, (size, size // 2), 0)
        coarse = lax.broadcasted_iota(jnp.int32, (size, size // 2), 1)
        return jnp.where((fine >> 1) == coarse, 1.0, 0.0).astype(jnp.bfloat16)

    def three(v):
        high = v.astype(jnp.bfloat16)
        rest = v - high.astype(jnp.float32)
        mid = rest.astype(jnp.bfloat16)
        low = (rest - mid.astype(jnp.float32)).astype(jnp.bfloat16)
        return [high, mid, low]

    def sum_pairs_z(v):
        rows, size = v.shape
        parts = jnp.concatenate(three(v), axis=0)
        got = jnp.dot(parts, pair_matrix(size), preferred_element_type=jnp.float32)
        return got[:rows] + got[rows : 2 * rows] + got[2 * rows :]

    def squeeze(level, sources, ways):
        nx, ny, nz = dims_of[level]
        tmp, cols = pair_t[level], cols_t[level]
        hx, hy = nx // 2, ny // 2
        kept = len(sources)
        odd = (lax.broadcasted_iota(jnp.int32, (1, 1, nz), 2) & 1) == 1
        for n, (source, way) in enumerate(zip(sources, ways)):
            for i in range(hx):
                v = source(2 * i + 1)
                if way != 0:
                    v = source(2 * i) + v
                tmp[n * hx + i : n * hx + i + 1] = v
            some = slice(n * hx, (n + 1) * hx)
            for j in range(hy):
                v = tmp[some, 2 * j + 1 : 2 * j + 2, :]
                if way != 1:
                    v = v + tmp[some, 2 * j : 2 * j + 1, :]
                if way == 2:
                    v = jnp.where(odd, v, 0.0)
                cols[some, j : j + 1, :] = v * (0.125 if way is None else 0.25)
        total = kept * hx
        flat = cols[0:total].reshape(total * 8, nz)
        got = sum_pairs_z(flat).reshape(total, 8, nz // 2)
        return [got[n * hx : (n + 1) * hx, 0:hy, :] for n in range(kept)]

    def coarse_coefs(level):
        these = per[level]
        names = ("a", "bx", "by", "bz")
        sources = [
            functools.partial(lambda ref, i: ref[i : i + 1], these[name]) for name in names
        ]
        for name, v in zip(names, squeeze(level, sources, (None, 0, 1, 2))):
            per[level + 1][name][...] = v

    for level in range(1, LEVELS):
        coarse_coefs(level - 1)
        put_lower(level)
        send(group_of("lower", level))

    def make_coefs(level):
        these = per[level]
        nx, ny, nz = dims_of[level]
        scale = 0.25**level
        lower_x = in_buf[("lower", level, (1, 0))]
        lower_y = in_buf[("lower", level, (0, 1))]
        pad = these["open"]
        last = lax.broadcasted_iota(jnp.int32, (nx, ny, nz), 2)
        bx, by, bz = these["bx"][...], these["by"][...], these["bz"][...]
        bxl = jnp.concatenate([lower_x[...], bx[:-1]], axis=0) if nx > 1 else lower_x[...]
        pad[1 : 1 + nx, ROW : ROW + ny, :] = by
        pad[1 : 1 + nx, ROW - 1 : ROW, :] = lower_y[...]
        byl = pad[1 : 1 + nx, ROW - 1 : ROW - 1 + ny, :]
        bzl = jnp.where(last == 0, 0.0, pltpu.roll(bz, 1, 2))
        diag = these["a"][...] + scale * ((bx + bxl) + (by + byl) + (bz + bzl))
        over = 1.0 / diag
        these["diag"][...] = diag
        over_s = over * scale
        these["xu"][...] = bx * over_s
        these["xl"][...] = bxl * over_s
        these["yu"][...] = by * over_s
        these["yl"][...] = byl * over_s
        these["zu"][...] = jnp.where(last == nz - 1, 0.0, bz * over_s)
        these["zl"][...] = bzl * over_s
        return over

    toward_name = {(1, 0): "xu", (-1, 0): "xl", (0, 1): "yu", (0, -1): "yl"}

    def end_ways(way):
        return ((way[0], -1), (way[0], 1)) if way[0] else ((-1, way[1]), (1, way[1]))

    def cross(way, corner):
        return (0, corner[1]) if way[0] else (corner[0], 0)

    def put_toward(level):
        these = per[level]
        dims = dims_of[level]
        nx, ny, nz = dims
        for way in FACES:
            xs, ys = at_side(dims, way)
            shape = layer_shape(dims, way)
            offset = (xs.start + ys.start) & 1
            out_buf[("toward", level, way)][...] = jnp.where(
                parity_at(shape, offset), these[toward_name[way]][xs, ys, :], 0.0
            )
            for n, corner in enumerate(end_ways(way)):
                cxs, cys = at_side(dims, corner)
                offset = (cxs.start + cys.start) & 1
                out_buf[("ends", level, way)][n] = jnp.where(
                    parity_at((1, 1, nz), offset),
                    these[toward_name[cross(way, corner)]][cxs, cys, :],
                    0.0,
                )
        send(group_of("toward", level) + group_of("ends", level))

    def sums(level, pad):
        these = per[level]
        nx, ny, nz = dims_of[level]
        own = pad[1 : 1 + nx, ROW : ROW + ny, :]
        total = these["g"][...]
        total = total + these["xu"][...] * pad[2 : 2 + nx, ROW : ROW + ny, :]
        total = total + these["xl"][...] * pad[0:nx, ROW : ROW + ny, :]
        total = total + these["yu"][...] * pad[1 : 1 + nx, ROW + 1 : ROW + 1 + ny, :]
        total = total + these["yl"][...] * pad[1 : 1 + nx, ROW - 1 : ROW - 1 + ny, :]
        total = total + these["zu"][...] * pltpu.roll(own, nz - 1, 2)
        total = total + these["zl"][...] * pltpu.roll(own, 1, 2)
        return own, total

    def half_sweep(level, half, red):
        these = per[level]
        dims = dims_of[level]
        nx, ny, nz = dims
        shut, pad = these["shut"], these["open"]
        kind = "half%d" % half
        black = parity_at(dims)
        shut[1 : 1 + nx, ROW : ROW + ny, :] = red
        _, total = sums(level, shut)
        value = jnp.where(black, total, red)
        pad[1 : 1 + nx, ROW : ROW + ny, :] = value
        group = group_of(kind, level)
        for key in group:
            xs, ys = at_side(dims, key[2])
            out_buf[key][...] = pad[
                xs.start + 1 : xs.stop + 1, ys.start + ROW : ys.stop + ROW, :
            ]
        send(group)

    def finish_half(level, half, last):
        these = per[level]
        dims = dims_of[level]
        nx, ny, nz = dims
        pad = these["open"]
        kind = "half%d" % half
        group = group_of(kind, level)
        receive(group)
        if half == 0:
            receive(group_of("toward", level) + group_of("ends", level))
        back = lambda way: (-way[0], -way[1])
        if not last:
            for way in FACES:
                xs, ys = at_side(dims, way)
                mine = out_buf[(kind, level, way)][...]
                theirs = in_buf[(kind, level, back(way))][...]
                theirs = theirs + in_buf[("toward", level, back(way))][...] * mine
                hx, hy = halo_place(dims, way)
                pad[hx, hy, :] = theirs
                ends = in_buf[("ends", level, back(way))]
                for n, corner in enumerate(end_ways(way)):
                    cx, cy = at_side(dims, corner)
                    px = hx if way[0] else slice(1 + cx.start, 1 + cx.stop)
                    py = hy if way[1] else slice(ROW + cy.start, ROW + cy.stop)
                    column = in_buf[(kind, level, back(corner))][...]
                    pad[px, py, :] = pad[px, py, :] + ends[n] * column
        for way in FACES:
            xs, ys = at_side(dims, way)
            px = slice(1 + xs.start, 1 + xs.stop)
            py = slice(ROW + ys.start, ROW + ys.stop)
            theirs = in_buf[(kind, level, back(way))][...]
            pad[px, py, :] = pad[px, py, :] + out_buf[("toward", level, way)][...] * theirs

    for level in range(LEVELS):
        these = per[level]
        nx, ny, nz = dims_of[level]
        these["shut"][...] = jnp.zeros(these["shut"].shape, jnp.float32)

    source = None
    for level in range(LEVELS):
        these = per[level]
        dims = dims_of[level]
        nx, ny, nz = dims
        pad = these["open"]
        red_cells = jnp.logical_not(parity_at(dims))
        if level == 0:
            receive(group_of("lower", 0))
            these["g"][...] = f_in[...] * make_coefs(0)
            receive(group_of("first", 0))
            pad[1 : 1 + nx, ROW : ROW + ny, :] = u_in[...]
            for way in FACES:
                hx, hy = halo_place(dims, way)
                pad[hx, hy, :] = in_buf[("first", 0, (-way[0], -way[1]))][...]
            own, total = sums(0, pad)
            half_sweep(0, 0, jnp.where(red_cells, total, own))
            put_toward(0)
            for other in range(1, LEVELS):
                receive(group_of("lower", other))
                per[other]["g"][...] = make_coefs(other)
                put_toward(other)
        else:
            these["g"][...] = source * these["g"][...]
            half_sweep(level, 0, jnp.where(red_cells, these["g"][...], 0.0))
        finish_half(level, 0, False)
        own, total = sums(level, pad)
        half_sweep(level, 1, jnp.where(red_cells, total, own))
        finish_half(level, 1, level == LEVELS - 1)
        outs[level][...] = pad[1 : 1 + nx, ROW : ROW + ny, :]
        if level + 1 < LEVELS:
            own, total = sums(level, pad)
            these["a"][...] = jnp.where(red_cells, these["diag"][...] * (total - own), 0.0)
            take = functools.partial(lambda ref, i: ref[i : i + 1], these["a"])
            source = squeeze(level, [take], (None,))[0]

    for way in AROUND:
        chosen = [key for key in keys if key[2] == way]

        @pl.when(inside(*way))
        def _():
            for key in chosen:
                copy_of(key).wait_send()


def shards(solution, right_side, alpha, beta_x, beta_y, beta_z):
    dims_of = [tuple(size >> level for size in solution.shape) for level in range(LEVELS)]
    found = messages(dims_of)
    keys = list(found)
    buffers = [pltpu.VMEM(found[key], jnp.float32) for key in keys]
    scratch = buffers + buffers
    for nx, ny, nz in dims_of:
        rows = 24 if ny + 1 > 8 else 16
        scratch += [pltpu.VMEM((nx + 2, rows, nz), jnp.float32)] * 2
        scratch += [pltpu.VMEM((nx, ny, nz), jnp.float32)] * 12
    for nx, ny, nz in dims_of[:2]:
        scratch += [pltpu.VMEM((4 * nx // 2, ny, nz), jnp.float32)]
    for nx, ny, nz in dims_of[:2]:
        scratch += [pltpu.VMEM((4 * nx // 2, 8, nz), jnp.float32)]
    scratch += [pltpu.SemaphoreType.DMA((len(keys),))] * 2
    return pl.pallas_call(
        functools.partial(kernel, dims_of, keys),
        out_shape=[jax.ShapeDtypeStruct(dims, jnp.float32) for dims in dims_of],
        in_specs=[pl.BlockSpec(memory_space=pltpu.VMEM)] * 6,
        out_specs=[pl.BlockSpec(memory_space=pltpu.VMEM)] * 3,
        scratch_shapes=scratch,
        compiler_params=pltpu.CompilerParams(
            collective_id=0, has_side_effects=True, vmem_limit_bytes=48 * 1024 * 1024
        ),
        name="vcycle",
    )(solution, right_side, alpha, beta_x, beta_y, beta_z)


def solution(mesh):
    place = P("gx", "gy", None)
    return jax.shard_map(
        shards,
        mesh=mesh,
        in_specs=(place,) * 6,
        out_specs=(place,) * 3,
        check_vma=False,
    )
```

```python
import functools

import jax
import jax.numpy as jnp
from jax import lax
from jax.experimental import pallas as pl
from jax.experimental.pallas import tpu as pltpu
from jax.sharding import PartitionSpec as P

LEVELS = 3
VMEM_LIMIT = (64 * 1024 - 160) * 1024
ROW = 8

FACES = ((1, 0), (-1, 0), (0, 1), (0, -1))
CORNERS = ((1, 1), (1, -1), (-1, 1), (-1, -1))
AROUND = FACES + CORNERS


def layer_shape(dims, way):
    nx, ny, nz = dims
    return (1 if way[0] else nx, 1 if way[1] else ny, nz)


def edge_shape(dims, way):
    return (2, 1, 1, dims[2])


def messages(dims_of):
    found = {}
    for way in FACES:
        found[("first", 0, way)] = layer_shape(dims_of[0], way)
    for level, dims in enumerate(dims_of):
        for way in ((1, 0), (0, 1)):
            found[("lower", level, way)] = layer_shape(dims, way)
        for way in FACES:
            found[("toward", level, way)] = layer_shape(dims, way)
            found[("ends", level, way)] = edge_shape(dims, way)
        for half in range(2):
            ways = FACES if (level == LEVELS - 1 and half == 1) else AROUND
            for way in ways:
                found[("half%d" % half, level, way)] = layer_shape(dims, way)
    return found


def at_side(dims, way):
    nx, ny, _ = dims
    xs = {0: slice(0, nx), 1: slice(nx - 1, nx), -1: slice(0, 1)}[way[0]]
    ys = {0: slice(0, ny), 1: slice(ny - 1, ny), -1: slice(0, 1)}[way[1]]
    return xs, ys


def halo_place(dims, way):
    nx, ny, _ = dims
    xs = {0: slice(1, 1 + nx), 1: slice(nx + 1, nx + 2), -1: slice(0, 1)}[way[0]]
    ys = {0: slice(ROW, ROW + ny), 1: slice(ROW + ny, ROW + ny + 1), -1: slice(ROW - 1, ROW)}[way[1]]
    return xs, ys


def parity_at(shape, offset=0):
    total = (
        lax.broadcasted_iota(jnp.int32, shape, 0)
        + lax.broadcasted_iota(jnp.int32, shape, 1)
        + lax.broadcasted_iota(jnp.int32, shape, 2)
        + offset
    )
    return (total & 1) == 1


def kernel(dims_of, keys, *refs):
    refs = list(refs)
    args = refs[:6]
    outs = refs[6:9]
    u_in, f_in, a_in, bx_in, by_in, bz_in = held = refs[9:15]
    load_sem, store_sem = refs[15:17]
    kept = refs[17:20]
    refs = refs[20:]
    n_keys = len(keys)
    out_buf = dict(zip(keys, refs[:n_keys]))
    in_buf = dict(zip(keys, refs[n_keys : 2 * n_keys]))
    refs = refs[2 * n_keys :]
    names = ("open", "shut", "g", "diag", "xu", "xl", "yu", "yl", "zu", "zl", "a", "bx", "by", "bz")
    per = []
    for level in range(LEVELS):
        per.append(dict(zip(names, refs[: len(names)])))
        refs = refs[len(names) :]
    pair_t, cols_t = refs[0:2], refs[2:4]
    send_sem, recv_sem = refs[4], refs[5]

    gx, gy = lax.axis_index("gx"), lax.axis_index("gy")
    n_x, n_y = lax.axis_size("gx"), lax.axis_size("gy")

    def inside(dx, dy):
        ok = None
        for place, step, count in ((gx, dx, n_x), (gy, dy, n_y)):
            if step == 0:
                continue
            here = (place + step < count) if step > 0 else (place + step >= 0)
            ok = here if ok is None else jnp.logical_and(ok, here)
        return ok

    def copy_of(key):
        way = key[2]
        index = keys.index(key)
        return pltpu.make_async_remote_copy(
            src_ref=out_buf[key],
            dst_ref=in_buf[key],
            send_sem=send_sem.at[index],
            recv_sem=recv_sem.at[index],
            device_id={"gx": gx + way[0], "gy": gy + way[1]},
            device_id_type=pl.DeviceIdType.MESH,
        )

    def send(group):
        for way in AROUND:
            chosen = [key for key in group if key[2] == way]
            if chosen:

                @pl.when(inside(*way))
                def _():
                    for key in chosen:
                        copy_of(key).start()

    def receive(group):
        for way in AROUND:
            chosen = [key for key in group if key[2] == way]
            if chosen:

                @pl.when(inside(-way[0], -way[1]))
                def _():
                    for key in chosen:
                        copy_of(key).wait_recv()

    def group_of(kind, level):
        return [key for key in keys if key[0] == kind and key[1] == level]

    stores = [pltpu.make_async_copy(kept[n], outs[n], store_sem.at[n]) for n in range(LEVELS)]
    loads = [pltpu.make_async_copy(args[n], held[n], load_sem.at[n]) for n in range(6)]

    barrier = pltpu.get_barrier_semaphore()
    for way in AROUND:

        @pl.when(inside(*way))
        def _():
            pl.semaphore_signal(
                barrier,
                inc=1,
                device_id={"gx": gx + way[0], "gy": gy + way[1]},
                device_id_type=pl.DeviceIdType.MESH,
            )

    for n in (0, 3, 4, 2, 5, 1):
        loads[n].start()

    def put_faces(kind, level, source, ways):
        for way in ways:
            xs, ys = at_side(dims_of[level], way)
            out_buf[(kind, level, way)][...] = source[xs, ys, :]

    loads[0].wait()
    put_faces("first", 0, u_in, FACES)

    def put_lower(level):
        for way, name in (((1, 0), "bx"), ((0, 1), "by")):
            xs, ys = at_side(dims_of[level], way)
            out_buf[("lower", level, way)][...] = per[level][name][xs, ys, :]

    loads[3].wait()
    per[0]["bx"][...] = bx_in[...].astype(jnp.float32)
    loads[4].wait()
    per[0]["by"][...] = by_in[...].astype(jnp.float32)
    put_lower(0)

    for way in AROUND:
        chosen = [key for key in keys if key[2] == way]

        @pl.when(jnp.logical_not(inside(-way[0], -way[1])))
        def _():
            for key in chosen:
                in_buf[key][...] = jnp.zeros(in_buf[key].shape, jnp.float32)

    beside_x = (gx > 0).astype(jnp.int32) + (gx + 1 < n_x).astype(jnp.int32)
    beside_y = (gy > 0).astype(jnp.int32) + (gy + 1 < n_y).astype(jnp.int32)
    pl.semaphore_wait(barrier, beside_x + beside_y + beside_x * beside_y)

    send(group_of("first", 0) + group_of("lower", 0))
    loads[2].wait()
    per[0]["a"][...] = a_in[...].astype(jnp.float32)
    loads[5].wait()
    per[0]["bz"][...] = bz_in[...].astype(jnp.float32)
    loads[1].wait()

    def pair_matrix(size):
        fine = lax.broadcasted_iota(jnp.int32, (size, size // 2), 0)
        coarse = lax.broadcasted_iota(jnp.int32, (size, size // 2), 1)
        return jnp.where((fine >> 1) == coarse, 1.0, 0.0).astype(jnp.bfloat16)

    def three(v):
        high = v.astype(jnp.bfloat16)
        rest = v - high.astype(jnp.float32)
        mid = rest.astype(jnp.bfloat16)
        low = (rest - mid.astype(jnp.float32)).astype(jnp.bfloat16)
        return [high, mid, low]

    def sum_pairs_z(v):
        rows, size = v.shape
        parts = jnp.concatenate(three(v), axis=0)
        got = jnp.dot(parts, pair_matrix(size), preferred_element_type=jnp.float32)
        return got[:rows] + got[rows : 2 * rows] + got[2 * rows :]

    def squeeze(level, sources, ways):
        nx, ny, nz = dims_of[level]
        tmp, cols = pair_t[level], cols_t[level]
        hx, hy = nx // 2, ny // 2
        kept = len(sources)
        odd = (lax.broadcasted_iota(jnp.int32, (1, 1, nz), 2) & 1) == 1
        for n, (source, way) in enumerate(zip(sources, ways)):
            for i in range(hx):
                v = source(2 * i + 1)
                if way != 0:
                    v = source(2 * i) + v
                tmp[n * hx + i : n * hx + i + 1] = v
            some = slice(n * hx, (n + 1) * hx)
            for j in range(hy):
                v = tmp[some, 2 * j + 1 : 2 * j + 2, :]
                if way != 1:
                    v = v + tmp[some, 2 * j : 2 * j + 1, :]
                if way == 2:
                    v = jnp.where(odd, v, 0.0)
                cols[some, j : j + 1, :] = v * (0.125 if way is None else 0.25)
        total = kept * hx
        flat = cols[0:total].reshape(total * 8, nz)
        got = sum_pairs_z(flat).reshape(total, 8, nz // 2)
        return [got[n * hx : (n + 1) * hx, 0:hy, :] for n in range(kept)]

    def coarse_coefs(level):
        these = per[level]
        names = ("a", "bx", "by", "bz")
        sources = [
            functools.partial(lambda ref, i: ref[i : i + 1], these[name]) for name in names
        ]
        for name, v in zip(names, squeeze(level, sources, (None, 0, 1, 2))):
            per[level + 1][name][...] = v

    for level in range(1, LEVELS):
        coarse_coefs(level - 1)
        put_lower(level)
        send(group_of("lower", level))

    def make_coefs(level):
        these = per[level]
        nx, ny, nz = dims_of[level]
        scale = 0.25**level
        lower_x = in_buf[("lower", level, (1, 0))]
        lower_y = in_buf[("lower", level, (0, 1))]
        pad = these["open"]
        last = lax.broadcasted_iota(jnp.int32, (nx, ny, nz), 2)
        bx, by, bz = these["bx"][...], these["by"][...], these["bz"][...]
        bxl = jnp.concatenate([lower_x[...], bx[:-1]], axis=0) if nx > 1 else lower_x[...]
        pad[1 : 1 + nx, ROW : ROW + ny, :] = by
        pad[1 : 1 + nx, ROW - 1 : ROW, :] = lower_y[...]
        byl = pad[1 : 1 + nx, ROW - 1 : ROW - 1 + ny, :]
        bzl = jnp.where(last == 0, 0.0, pltpu.roll(bz, 1, 2))
        diag = these["a"][...] + scale * ((bx + bxl) + (by + byl) + (bz + bzl))
        over = 1.0 / diag
        these["diag"][...] = diag
        over_s = over * scale
        these["xu"][...] = bx * over_s
        these["xl"][...] = bxl * over_s
        these["yu"][...] = by * over_s
        these["yl"][...] = byl * over_s
        these["zu"][...] = jnp.where(last == nz - 1, 0.0, bz * over_s)
        these["zl"][...] = bzl * over_s
        return over

    toward_name = {(1, 0): "xu", (-1, 0): "xl", (0, 1): "yu", (0, -1): "yl"}

    def end_ways(way):
        return ((way[0], -1), (way[0], 1)) if way[0] else ((-1, way[1]), (1, way[1]))

    def cross(way, corner):
        return (0, corner[1]) if way[0] else (corner[0], 0)

    def put_toward(level):
        these = per[level]
        dims = dims_of[level]
        nx, ny, nz = dims
        for way in FACES:
            xs, ys = at_side(dims, way)
            shape = layer_shape(dims, way)
            offset = (xs.start + ys.start) & 1
            out_buf[("toward", level, way)][...] = jnp.where(
                parity_at(shape, offset), these[toward_name[way]][xs, ys, :], 0.0
            )
            for n, corner in enumerate(end_ways(way)):
                cxs, cys = at_side(dims, corner)
                offset = (cxs.start + cys.start) & 1
                out_buf[("ends", level, way)][n] = jnp.where(
                    parity_at((1, 1, nz), offset),
                    these[toward_name[cross(way, corner)]][cxs, cys, :],
                    0.0,
                )
        send(group_of("toward", level) + group_of("ends", level))

    def sums(level, pad):
        these = per[level]
        nx, ny, nz = dims_of[level]
        own = pad[1 : 1 + nx, ROW : ROW + ny, :]
        total = these["g"][...]
        total = total + these["xu"][...] * pad[2 : 2 + nx, ROW : ROW + ny, :]
        total = total + these["xl"][...] * pad[0:nx, ROW : ROW + ny, :]
        total = total + these["yu"][...] * pad[1 : 1 + nx, ROW + 1 : ROW + 1 + ny, :]
        total = total + these["yl"][...] * pad[1 : 1 + nx, ROW - 1 : ROW - 1 + ny, :]
        total = total + these["zu"][...] * pltpu.roll(own, nz - 1, 2)
        total = total + these["zl"][...] * pltpu.roll(own, 1, 2)
        return own, total

    def half_sweep(level, half, red):
        these = per[level]
        dims = dims_of[level]
        nx, ny, nz = dims
        shut, pad = these["shut"], these["open"]
        kind = "half%d" % half
        black = parity_at(dims)
        shut[1 : 1 + nx, ROW : ROW + ny, :] = red
        _, total = sums(level, shut)
        value = jnp.where(black, total, red)
        pad[1 : 1 + nx, ROW : ROW + ny, :] = value
        group = group_of(kind, level)
        for key in group:
            xs, ys = at_side(dims, key[2])
            out_buf[key][...] = pad[
                xs.start + 1 : xs.stop + 1, ys.start + ROW : ys.stop + ROW, :
            ]
        send(group)

    def finish_half(level, half, last):
        these = per[level]
        dims = dims_of[level]
        nx, ny, nz = dims
        pad = these["open"]
        kind = "half%d" % half
        group = group_of(kind, level)
        receive(group)
        if half == 0:
            receive(group_of("toward", level) + group_of("ends", level))
        back = lambda way: (-way[0], -way[1])
        if not last:
            for way in FACES:
                xs, ys = at_side(dims, way)
                mine = out_buf[(kind, level, way)][...]
                theirs = in_buf[(kind, level, back(way))][...]
                theirs = theirs + in_buf[("toward", level, back(way))][...] * mine
                hx, hy = halo_place(dims, way)
                pad[hx, hy, :] = theirs
                ends = in_buf[("ends", level, back(way))]
                for n, corner in enumerate(end_ways(way)):
                    cx, cy = at_side(dims, corner)
                    px = hx if way[0] else slice(1 + cx.start, 1 + cx.stop)
                    py = hy if way[1] else slice(ROW + cy.start, ROW + cy.stop)
                    column = in_buf[(kind, level, back(corner))][...]
                    pad[px, py, :] = pad[px, py, :] + ends[n] * column
        for way in FACES:
            xs, ys = at_side(dims, way)
            px = slice(1 + xs.start, 1 + xs.stop)
            py = slice(ROW + ys.start, ROW + ys.stop)
            theirs = in_buf[(kind, level, back(way))][...]
            pad[px, py, :] = pad[px, py, :] + out_buf[("toward", level, way)][...] * theirs

    for level in range(LEVELS):
        these = per[level]
        nx, ny, nz = dims_of[level]
        these["shut"][...] = jnp.zeros(these["shut"].shape, jnp.float32)

    source = None
    for level in range(LEVELS):
        these = per[level]
        dims = dims_of[level]
        nx, ny, nz = dims
        pad = these["open"]
        red_cells = jnp.logical_not(parity_at(dims))
        if level == 0:
            receive(group_of("lower", 0))
            these["g"][...] = f_in[...] * make_coefs(0)
            receive(group_of("first", 0))
            pad[1 : 1 + nx, ROW : ROW + ny, :] = u_in[...]
            for way in FACES:
                hx, hy = halo_place(dims, way)
                pad[hx, hy, :] = in_buf[("first", 0, (-way[0], -way[1]))][...]
            own, total = sums(0, pad)
            half_sweep(0, 0, jnp.where(red_cells, total, own))
            put_toward(0)
            for other in range(1, LEVELS):
                receive(group_of("lower", other))
                per[other]["g"][...] = make_coefs(other)
                put_toward(other)
        else:
            these["g"][...] = source * these["g"][...]
            half_sweep(level, 0, jnp.where(red_cells, these["g"][...], 0.0))
        finish_half(level, 0, False)
        own, total = sums(level, pad)
        half_sweep(level, 1, jnp.where(red_cells, total, own))
        finish_half(level, 1, level == LEVELS - 1)
        kept[level][...] = pad[1 : 1 + nx, ROW : ROW + ny, :]
        stores[level].start()
        if level + 1 < LEVELS:
            own, total = sums(level, pad)
            these["a"][...] = jnp.where(red_cells, these["diag"][...] * (total - own), 0.0)
            take = functools.partial(lambda ref, i: ref[i : i + 1], these["a"])
            source = squeeze(level, [take], (None,))[0]

    for way in AROUND:
        chosen = [key for key in keys if key[2] == way]

        @pl.when(inside(*way))
        def _():
            for key in chosen:
                copy_of(key).wait_send()

    for copy in stores:
        copy.wait()


def store(fine, middle, coarse, fine_out, middle_out, coarse_out, sem):
    pairs = ((fine, fine_out), (middle, middle_out), (coarse, coarse_out))
    copies = [pltpu.make_async_copy(src, dst, sem.at[n]) for n, (src, dst) in enumerate(pairs)]
    for copy in copies:
        copy.start()
    for copy in copies:
        copy.wait()


def shards(solution, right_side, alpha, beta_x, beta_y, beta_z):
    dims_of = [tuple(size >> level for size in solution.shape) for level in range(LEVELS)]
    found = messages(dims_of)
    keys = list(found)
    buffers = [pltpu.VMEM(found[key], jnp.float32) for key in keys]
    fine = dims_of[0]
    scratch = [pltpu.VMEM(fine, jnp.float32)] * 2 + [pltpu.VMEM(fine, jnp.bfloat16)] * 4
    scratch += [pltpu.SemaphoreType.DMA((6,)), pltpu.SemaphoreType.DMA((LEVELS,))]
    scratch += [pltpu.VMEM(dims, jnp.float32) for dims in dims_of]
    scratch += buffers + buffers
    for nx, ny, nz in dims_of:
        rows = 24 if ny + 1 > 8 else 16
        scratch += [pltpu.VMEM((nx + 2, rows, nz), jnp.float32)] * 2
        scratch += [pltpu.VMEM((nx, ny, nz), jnp.float32)] * 12
    for nx, ny, nz in dims_of[:2]:
        scratch += [pltpu.VMEM((4 * nx // 2, ny, nz), jnp.float32)]
    for nx, ny, nz in dims_of[:2]:
        scratch += [pltpu.VMEM((4 * nx // 2, 8, nz), jnp.float32)]
    scratch += [pltpu.SemaphoreType.DMA((len(keys),))] * 2
    iterates = pl.pallas_call(
        functools.partial(kernel, dims_of, keys),
        out_shape=[jax.ShapeDtypeStruct(dims, jnp.float32) for dims in dims_of],
        in_specs=[pl.BlockSpec(memory_space=pltpu.HBM)] * 6,
        out_specs=[pl.BlockSpec(memory_space=pltpu.HBM)] * 3,
        scratch_shapes=scratch,
        compiler_params=pltpu.CompilerParams(
            collective_id=0, has_side_effects=True, vmem_limit_bytes=VMEM_LIMIT
        ),
        name="vcycle",
    )(solution, right_side, alpha, beta_x, beta_y, beta_z)
    return pl.pallas_call(
        store,
        out_shape=[jax.ShapeDtypeStruct(dims, jnp.float32) for dims in dims_of],
        in_specs=[pl.BlockSpec(memory_space=pltpu.HBM)] * 3,
        out_specs=[pl.BlockSpec(memory_space=pltpu.HBM)] * 3,
        scratch_shapes=[pltpu.SemaphoreType.DMA((3,))],
        compiler_params=pltpu.CompilerParams(vmem_limit_bytes=VMEM_LIMIT),
        name="store",
    )(*iterates)


def solution(mesh):
    place = P("gx", "gy", None)
    return jax.shard_map(
        shards,
        mesh=mesh,
        in_specs=(place,) * 6,
        out_specs=(place,) * 3,
        check_vma=False,
    )
```

```python
import functools

import jax
import jax.numpy as jnp
from jax import lax
from jax.experimental import pallas as pl
from jax.experimental.pallas import tpu as pltpu
from jax.sharding import PartitionSpec as P

LEVELS = 3
VMEM_LIMIT = (64 * 1024 - 160) * 1024
ROW = 8

FACES = ((1, 0), (-1, 0), (0, 1), (0, -1))
CORNERS = ((1, 1), (1, -1), (-1, 1), (-1, -1))
AROUND = FACES + CORNERS
WIDE = AROUND + ((2, 0), (-2, 0), (0, 2), (0, -2))


def layer_shape(dims, way):
    nx, ny, nz = dims
    return (1 if way[0] else nx, 1 if way[1] else ny, nz)


def edge_shape(dims, way):
    return (2, 1, 1, dims[2])


def messages(dims_of):
    found = {}
    for way in FACES:
        found[("first", 0, way)] = layer_shape(dims_of[0], way)
    for way in WIDE:
        found[("raw", LEVELS - 1, way)] = (16, dims_of[-1][2])
        found[("source", LEVELS - 1, way)] = (8, dims_of[-1][2])
    for level, dims in enumerate(dims_of[:-1]):
        for way in ((1, 0), (0, 1)):
            found[("lower", level, way)] = layer_shape(dims, way)
        for way in FACES:
            found[("toward", level, way)] = layer_shape(dims, way)
            found[("ends", level, way)] = edge_shape(dims, way)
        for half in range(2):
            for way in AROUND:
                found[("half%d" % half, level, way)] = layer_shape(dims, way)
    return found


def at_side(dims, way):
    nx, ny, _ = dims
    xs = {0: slice(0, nx), 1: slice(nx - 1, nx), -1: slice(0, 1)}[way[0]]
    ys = {0: slice(0, ny), 1: slice(ny - 1, ny), -1: slice(0, 1)}[way[1]]
    return xs, ys


def halo_place(dims, way):
    nx, ny, _ = dims
    xs = {0: slice(1, 1 + nx), 1: slice(nx + 1, nx + 2), -1: slice(0, 1)}[way[0]]
    ys = {0: slice(ROW, ROW + ny), 1: slice(ROW + ny, ROW + ny + 1), -1: slice(ROW - 1, ROW)}[way[1]]
    return xs, ys


def parity_at(shape, offset=0):
    total = (
        lax.broadcasted_iota(jnp.int32, shape, 0)
        + lax.broadcasted_iota(jnp.int32, shape, 1)
        + lax.broadcasted_iota(jnp.int32, shape, 2)
        + offset
    )
    return (total & 1) == 1


def kernel(dims_of, keys, *refs):
    refs = list(refs)
    args = refs[:6]
    outs = refs[6:9]
    u_in, f_in, a_in, bx_in, by_in, bz_in = held = refs[9:15]
    load_sem, store_sem = refs[15:17]
    kept = refs[17:20]
    refs = refs[20:]
    n_keys = len(keys)
    out_buf = dict(zip(keys, refs[:n_keys]))
    in_buf = dict(zip(keys, refs[n_keys : 2 * n_keys]))
    refs = refs[2 * n_keys :]
    names = ("open", "shut", "g", "diag", "xu", "xl", "yu", "yl", "zu", "zl", "a", "bx", "by", "bz")
    per = []
    for level in range(LEVELS):
        per.append(dict(zip(names, refs[: len(names)])))
        refs = refs[len(names) :]
    pair_t, cols_t = refs[0:2], refs[2:4]
    send_sem, recv_sem = refs[4], refs[5]
    wide = dict(zip(("a", "bx", "by", "bz", "g", "over", "xu", "xl", "yu", "yl", "zu", "zl"), refs[6:]))

    gx, gy = lax.axis_index("gx"), lax.axis_index("gy")
    n_x, n_y = lax.axis_size("gx"), lax.axis_size("gy")

    def inside(dx, dy):
        ok = None
        for place, step, count in ((gx, dx, n_x), (gy, dy, n_y)):
            if step == 0:
                continue
            here = (place + step < count) if step > 0 else (place + step >= 0)
            ok = here if ok is None else jnp.logical_and(ok, here)
        return ok

    def copy_of(key):
        way = key[2]
        index = keys.index(key)
        shared = key[0] in ("raw", "source")
        return pltpu.make_async_remote_copy(
            src_ref=out_buf[key[:2] + WIDE[:1] if shared else key],
            dst_ref=in_buf[key],
            send_sem=send_sem.at[index],
            recv_sem=recv_sem.at[index],
            device_id={"gx": gx + way[0], "gy": gy + way[1]},
            device_id_type=pl.DeviceIdType.MESH,
        )

    def send(group):
        for way in WIDE:
            chosen = [key for key in group if key[2] == way]
            if chosen:

                @pl.when(inside(*way))
                def _():
                    for key in chosen:
                        copy_of(key).start()

    def receive(group):
        for way in WIDE:
            chosen = [key for key in group if key[2] == way]
            if chosen:

                @pl.when(inside(-way[0], -way[1]))
                def _():
                    for key in chosen:
                        copy_of(key).wait_recv()

    def group_of(kind, level):
        return [key for key in keys if key[0] == kind and key[1] == level]

    stores = [pltpu.make_async_copy(kept[n], outs[n], store_sem.at[n]) for n in range(LEVELS)]
    loads = [pltpu.make_async_copy(args[n], held[n], load_sem.at[n]) for n in range(6)]

    barrier = pltpu.get_barrier_semaphore()
    for way in WIDE:

        @pl.when(inside(*way))
        def _():
            pl.semaphore_signal(
                barrier,
                inc=1,
                device_id={"gx": gx + way[0], "gy": gy + way[1]},
                device_id_type=pl.DeviceIdType.MESH,
            )

    for n in (0, 3, 4, 2, 5, 1):
        loads[n].start()

    def put_faces(kind, level, source, ways):
        for way in ways:
            xs, ys = at_side(dims_of[level], way)
            out_buf[(kind, level, way)][...] = source[xs, ys, :]

    loads[0].wait()
    put_faces("first", 0, u_in, FACES)

    def put_lower(level):
        for way, name in (((1, 0), "bx"), ((0, 1), "by")):
            xs, ys = at_side(dims_of[level], way)
            out_buf[("lower", level, way)][...] = per[level][name][xs, ys, :]

    loads[3].wait()
    per[0]["bx"][...] = bx_in[...].astype(jnp.float32)
    loads[4].wait()
    per[0]["by"][...] = by_in[...].astype(jnp.float32)
    put_lower(0)

    for way in AROUND:
        chosen = [key for key in keys if key[2] == way and key[0] not in ("raw", "source")]

        @pl.when(jnp.logical_not(inside(-way[0], -way[1])))
        def _():
            for key in chosen:
                in_buf[key][...] = jnp.zeros(in_buf[key].shape, jnp.float32)

    beside_x = (gx > 0).astype(jnp.int32) + (gx + 1 < n_x).astype(jnp.int32)
    beside_y = (gy > 0).astype(jnp.int32) + (gy + 1 < n_y).astype(jnp.int32)
    far_x = (gx > 1).astype(jnp.int32) + (gx + 2 < n_x).astype(jnp.int32)
    far_y = (gy > 1).astype(jnp.int32) + (gy + 2 < n_y).astype(jnp.int32)
    pl.semaphore_wait(barrier, beside_x + beside_y + beside_x * beside_y + far_x + far_y)

    send(group_of("first", 0) + group_of("lower", 0))
    loads[2].wait()
    per[0]["a"][...] = a_in[...].astype(jnp.float32)
    loads[5].wait()
    per[0]["bz"][...] = bz_in[...].astype(jnp.float32)
    loads[1].wait()

    def pair_matrix(size):
        fine = lax.broadcasted_iota(jnp.int32, (size, size // 2), 0)
        coarse = lax.broadcasted_iota(jnp.int32, (size, size // 2), 1)
        return jnp.where((fine >> 1) == coarse, 1.0, 0.0).astype(jnp.bfloat16)

    def three(v):
        high = v.astype(jnp.bfloat16)
        rest = v - high.astype(jnp.float32)
        mid = rest.astype(jnp.bfloat16)
        low = (rest - mid.astype(jnp.float32)).astype(jnp.bfloat16)
        return [high, mid, low]

    def sum_pairs_z(v):
        rows, size = v.shape
        parts = jnp.concatenate(three(v), axis=0)
        got = jnp.dot(parts, pair_matrix(size), preferred_element_type=jnp.float32)
        return got[:rows] + got[rows : 2 * rows] + got[2 * rows :]

    def squeeze(level, sources, ways):
        nx, ny, nz = dims_of[level]
        tmp, cols = pair_t[level], cols_t[level]
        hx, hy = nx // 2, ny // 2
        kept = len(sources)
        odd = (lax.broadcasted_iota(jnp.int32, (1, 1, nz), 2) & 1) == 1
        for n, (source, way) in enumerate(zip(sources, ways)):
            for i in range(hx):
                v = source(2 * i + 1)
                if way != 0:
                    v = source(2 * i) + v
                tmp[n * hx + i : n * hx + i + 1] = v
            some = slice(n * hx, (n + 1) * hx)
            for j in range(hy):
                v = tmp[some, 2 * j + 1 : 2 * j + 2, :]
                if way != 1:
                    v = v + tmp[some, 2 * j : 2 * j + 1, :]
                if way == 2:
                    v = jnp.where(odd, v, 0.0)
                cols[some, j : j + 1, :] = v * (0.125 if way is None else 0.25)
        total = kept * hx
        flat = cols[0:total].reshape(total * 8, nz)
        got = sum_pairs_z(flat).reshape(total, 8, nz // 2)
        return [got[n * hx : (n + 1) * hx, 0:hy, :] for n in range(kept)]

    def coarse_coefs(level):
        these = per[level]
        names = ("a", "bx", "by", "bz")
        sources = [
            functools.partial(lambda ref, i: ref[i : i + 1], these[name]) for name in names
        ]
        for name, v in zip(names, squeeze(level, sources, (None, 0, 1, 2))):
            per[level + 1][name][...] = v

    def prepare_coarse():
        coarse_coefs(0)
        put_lower(1)
        send(group_of("lower", 1))
        coarse_coefs(1)
        put_raw()

    def make_coefs(level):
        these = per[level]
        nx, ny, nz = dims_of[level]
        scale = 0.25**level
        lower_x = in_buf[("lower", level, (1, 0))]
        lower_y = in_buf[("lower", level, (0, 1))]
        pad = these["open"]
        last = lax.broadcasted_iota(jnp.int32, (nx, ny, nz), 2)
        bx, by, bz = these["bx"][...], these["by"][...], these["bz"][...]
        bxl = jnp.concatenate([lower_x[...], bx[:-1]], axis=0) if nx > 1 else lower_x[...]
        pad[1 : 1 + nx, ROW : ROW + ny, :] = by
        pad[1 : 1 + nx, ROW - 1 : ROW, :] = lower_y[...]
        byl = pad[1 : 1 + nx, ROW - 1 : ROW - 1 + ny, :]
        bzl = jnp.where(last == 0, 0.0, pltpu.roll(bz, 1, 2))
        diag = these["a"][...] + scale * ((bx + bxl) + (by + byl) + (bz + bzl))
        over = 1.0 / diag
        these["diag"][...] = diag
        over_s = over * scale
        these["xu"][...] = bx * over_s
        these["xl"][...] = bxl * over_s
        these["yu"][...] = by * over_s
        these["yl"][...] = byl * over_s
        these["zu"][...] = jnp.where(last == nz - 1, 0.0, bz * over_s)
        these["zl"][...] = bzl * over_s
        return over

    toward_name = {(1, 0): "xu", (-1, 0): "xl", (0, 1): "yu", (0, -1): "yl"}

    def end_ways(way):
        return ((way[0], -1), (way[0], 1)) if way[0] else ((-1, way[1]), (1, way[1]))

    def cross(way, corner):
        return (0, corner[1]) if way[0] else (corner[0], 0)

    def put_toward(level):
        these = per[level]
        dims = dims_of[level]
        nx, ny, nz = dims
        for way in FACES:
            xs, ys = at_side(dims, way)
            shape = layer_shape(dims, way)
            offset = (xs.start + ys.start) & 1
            out_buf[("toward", level, way)][...] = jnp.where(
                parity_at(shape, offset), these[toward_name[way]][xs, ys, :], 0.0
            )
            for n, corner in enumerate(end_ways(way)):
                cxs, cys = at_side(dims, corner)
                offset = (cxs.start + cys.start) & 1
                out_buf[("ends", level, way)][n] = jnp.where(
                    parity_at((1, 1, nz), offset),
                    these[toward_name[cross(way, corner)]][cxs, cys, :],
                    0.0,
                )
        send(group_of("toward", level) + group_of("ends", level))

    def sums(level, pad):
        these = per[level]
        nx, ny, nz = dims_of[level]
        own = pad[1 : 1 + nx, ROW : ROW + ny, :]
        total = these["g"][...]
        total = total + these["xu"][...] * pad[2 : 2 + nx, ROW : ROW + ny, :]
        total = total + these["xl"][...] * pad[0:nx, ROW : ROW + ny, :]
        total = total + these["yu"][...] * pad[1 : 1 + nx, ROW + 1 : ROW + 1 + ny, :]
        total = total + these["yl"][...] * pad[1 : 1 + nx, ROW - 1 : ROW - 1 + ny, :]
        total = total + these["zu"][...] * pltpu.roll(own, nz - 1, 2)
        total = total + these["zl"][...] * pltpu.roll(own, 1, 2)
        return own, total

    def half_sweep(level, half, red):
        these = per[level]
        dims = dims_of[level]
        nx, ny, nz = dims
        shut, pad = these["shut"], these["open"]
        kind = "half%d" % half
        black = parity_at(dims)
        shut[1 : 1 + nx, ROW : ROW + ny, :] = red
        _, total = sums(level, shut)
        value = jnp.where(black, total, red)
        pad[1 : 1 + nx, ROW : ROW + ny, :] = value
        group = group_of(kind, level)
        for key in group:
            xs, ys = at_side(dims, key[2])
            out_buf[key][...] = pad[
                xs.start + 1 : xs.stop + 1, ys.start + ROW : ys.stop + ROW, :
            ]
        send(group)

    def finish_half(level, half, last):
        these = per[level]
        dims = dims_of[level]
        nx, ny, nz = dims
        pad = these["open"]
        kind = "half%d" % half
        group = group_of(kind, level)
        receive(group)
        if half == 0:
            receive(group_of("toward", level) + group_of("ends", level))
        back = lambda way: (-way[0], -way[1])
        if not last:
            for way in FACES:
                xs, ys = at_side(dims, way)
                mine = out_buf[(kind, level, way)][...]
                theirs = in_buf[(kind, level, back(way))][...]
                theirs = theirs + in_buf[("toward", level, back(way))][...] * mine
                hx, hy = halo_place(dims, way)
                pad[hx, hy, :] = theirs
                ends = in_buf[("ends", level, back(way))]
                for n, corner in enumerate(end_ways(way)):
                    cx, cy = at_side(dims, corner)
                    px = hx if way[0] else slice(1 + cx.start, 1 + cx.stop)
                    py = hy if way[1] else slice(ROW + cy.start, ROW + cy.stop)
                    column = in_buf[(kind, level, back(corner))][...]
                    pad[px, py, :] = pad[px, py, :] + ends[n] * column
        for way in FACES:
            xs, ys = at_side(dims, way)
            px = slice(1 + xs.start, 1 + xs.stop)
            py = slice(ROW + ys.start, ROW + ys.stop)
            theirs = in_buf[(kind, level, back(way))][...]
            pad[px, py, :] = pad[px, py, :] + out_buf[("toward", level, way)][...] * theirs

    last = LEVELS - 1
    wide_names = ("a", "bx", "by", "bz")

    def put_raw():
        buffer = out_buf[("raw", last, WIDE[0])]
        for c, name in enumerate(wide_names):
            for x in range(2):
                buffer[4 * c + 2 * x : 4 * c + 2 * x + 2, :] = per[last][name][x]
        send(group_of("raw", last))

    def spread(kind, targets):
        for way in WIDE:
            key = (kind, last, way)
            at = (-2 * way[0], -2 * way[1])

            @pl.when(inside(-way[0], -way[1]))
            def _():
                copy_of(key).wait_recv()
                for c, target in enumerate(targets):
                    for x in range(2):
                        if not -3 <= at[0] + x <= 4:
                            continue
                        ys = [y for y in range(2) if -3 <= at[1] + y <= 4]
                        row = 4 * c + 2 * x + ys[0]
                        to = (at[1] + ys[0]) % 8
                        target[at[0] + x + 3, to : to + len(ys), :] = in_buf[key][
                            row : row + len(ys), :
                        ]

    def lower_x(v):
        return jnp.concatenate([jnp.zeros_like(v[:1]), v[:-1]], axis=0)

    def upper_x(v):
        return jnp.concatenate([v[1:], jnp.zeros_like(v[:1])], axis=0)

    def wide_coefs():
        scale = 0.25**last
        nz = dims_of[last][2]
        for name in wide_names:
            wide[name][...] = jnp.zeros(wide[name].shape, jnp.float32)
            wide[name][3:5, 0:2, :] = per[last][name][...]
        wide["g"][...] = jnp.zeros(wide["g"].shape, jnp.float32)
        spread("raw", [wide[name] for name in wide_names])
        a, bx, by, bz = (wide[name][...] for name in wide_names)
        place = lax.broadcasted_iota(jnp.int32, a.shape, 2)
        bxl, byl = lower_x(bx), pltpu.roll(by, 1, 1)
        bzl = jnp.where(place == 0, 0.0, pltpu.roll(bz, 1, 2))
        diag = a + scale * ((bx + bxl) + (by + byl) + (bz + bzl))
        over = jnp.where(a > 0.0, 1.0 / jnp.where(a > 0.0, diag, 1.0), 0.0)
        wide["over"][...] = over
        over = over * scale
        wide["xu"][...], wide["xl"][...] = bx * over, bxl * over
        wide["yu"][...], wide["yl"][...] = by * over, byl * over
        wide["zu"][...] = jnp.where(place == nz - 1, 0.0, bz * over)
        wide["zl"][...] = bzl * over

    def wide_level(source):
        nz = dims_of[last][2]
        own = source * wide["over"][3:5, 0:2, :]
        buffer = out_buf[("source", last, WIDE[0])]
        for x in range(2):
            buffer[2 * x : 2 * x + 2, :] = own[x]
        send(group_of("source", last))
        wide["g"][3:5, 0:2, :] = own
        spread("source", [wide["g"]])
        g = wide["g"][...]
        black = parity_at(g.shape, 1)
        u = jnp.where(black, 0.0, g)
        for step in range(3):
            total = g + wide["xu"][...] * upper_x(u) + wide["xl"][...] * lower_x(u)
            total = total + wide["yu"][...] * pltpu.roll(u, 7, 1)
            total = total + wide["yl"][...] * pltpu.roll(u, 1, 1)
            total = total + wide["zu"][...] * pltpu.roll(u, nz - 1, 2)
            total = total + wide["zl"][...] * pltpu.roll(u, 1, 2)
            u = jnp.where(black, u, total) if step == 1 else jnp.where(black, total, u)
        kept[last][...] = u[3:5, 0:2, :]
        stores[last].start()

    for level in range(last):
        per[level]["shut"][...] = jnp.zeros(per[level]["shut"].shape, jnp.float32)

    source = None
    for level in range(last):
        these = per[level]
        dims = dims_of[level]
        nx, ny, nz = dims
        pad = these["open"]
        red_cells = jnp.logical_not(parity_at(dims))
        if level == 0:
            receive(group_of("lower", 0))
            these["g"][...] = f_in[...] * make_coefs(0)
            receive(group_of("first", 0))
            pad[1 : 1 + nx, ROW : ROW + ny, :] = u_in[...]
            for way in FACES:
                hx, hy = halo_place(dims, way)
                pad[hx, hy, :] = in_buf[("first", 0, (-way[0], -way[1]))][...]
            own, total = sums(0, pad)
            half_sweep(0, 0, jnp.where(red_cells, total, own))
            put_toward(0)
            prepare_coarse()
        else:
            these["g"][...] = source * these["g"][...]
            half_sweep(level, 0, jnp.where(red_cells, these["g"][...], 0.0))
            wide_coefs()
        finish_half(level, 0, False)
        own, total = sums(level, pad)
        half_sweep(level, 1, jnp.where(red_cells, total, own))
        if level == 0:
            receive(group_of("lower", 1))
            per[1]["g"][...] = make_coefs(1)
            put_toward(1)
        finish_half(level, 1, False)
        kept[level][...] = pad[1 : 1 + nx, ROW : ROW + ny, :]
        stores[level].start()
        own, total = sums(level, pad)
        these["a"][...] = jnp.where(red_cells, these["diag"][...] * (total - own), 0.0)
        take = functools.partial(lambda ref, i: ref[i : i + 1], these["a"])
        source = squeeze(level, [take], (None,))[0]
    wide_level(source)

    for way in WIDE:
        chosen = [key for key in keys if key[2] == way]

        @pl.when(inside(*way))
        def _():
            for key in chosen:
                copy_of(key).wait_send()

    for copy in stores:
        copy.wait()


def store(*refs):
    given, outs, held, sem = refs[:3], refs[3:6], refs[6:9], refs[9]
    loads = [pltpu.make_async_copy(given[n], held[n], sem.at[n]) for n in range(3)]
    stores = [pltpu.make_async_copy(held[n], outs[n], sem.at[3 + n]) for n in range(3)]
    for copy in loads:
        copy.start()
    for load, copy in zip(loads, stores):
        load.wait()
        copy.start()
    for copy in stores:
        copy.wait()


def shards(solution, right_side, alpha, beta_x, beta_y, beta_z):
    dims_of = [tuple(size >> level for size in solution.shape) for level in range(LEVELS)]
    found = messages(dims_of)
    keys = list(found)
    buffers = [pltpu.VMEM(found[key], jnp.float32) for key in keys]
    fine = dims_of[0]
    scratch = [pltpu.VMEM(fine, jnp.float32)] * 2 + [pltpu.VMEM(fine, jnp.bfloat16)] * 4
    scratch += [pltpu.SemaphoreType.DMA((6,)), pltpu.SemaphoreType.DMA((LEVELS,))]
    scratch += [pltpu.VMEM(dims, jnp.float32) for dims in dims_of]
    scratch += buffers + buffers
    for nx, ny, nz in dims_of:
        rows = 24 if ny + 1 > 8 else 16
        scratch += [pltpu.VMEM((nx + 2, rows, nz), jnp.float32)] * 2
        scratch += [pltpu.VMEM((nx, ny, nz), jnp.float32)] * 12
    for nx, ny, nz in dims_of[:2]:
        scratch += [pltpu.VMEM((4 * nx // 2, ny, nz), jnp.float32)]
    for nx, ny, nz in dims_of[:2]:
        scratch += [pltpu.VMEM((4 * nx // 2, 8, nz), jnp.float32)]
    scratch += [pltpu.SemaphoreType.DMA((len(keys),))] * 2
    scratch += [pltpu.VMEM((8, 8, dims_of[-1][2]), jnp.float32)] * 12
    iterates = pl.pallas_call(
        functools.partial(kernel, dims_of, keys),
        out_shape=[jax.ShapeDtypeStruct(dims, jnp.float32) for dims in dims_of],
        in_specs=[pl.BlockSpec(memory_space=pltpu.HBM)] * 6,
        out_specs=[pl.BlockSpec(memory_space=pltpu.HBM)] * 3,
        scratch_shapes=scratch,
        compiler_params=pltpu.CompilerParams(
            collective_id=0, has_side_effects=True, vmem_limit_bytes=VMEM_LIMIT
        ),
        name="vcycle",
    )(solution, right_side, alpha, beta_x, beta_y, beta_z)
    return pl.pallas_call(
        store,
        out_shape=[jax.ShapeDtypeStruct(dims, jnp.float32) for dims in dims_of],
        in_specs=[pl.BlockSpec(memory_space=pltpu.HBM)] * 3,
        out_specs=[pl.BlockSpec(memory_space=pltpu.HBM)] * 3,
        scratch_shapes=[pltpu.VMEM(dims, jnp.float32) for dims in dims_of]
        + [pltpu.SemaphoreType.DMA((6,))],
        compiler_params=pltpu.CompilerParams(vmem_limit_bytes=VMEM_LIMIT),
        name="store",
    )(*iterates)


def solution(mesh):
    place = P("gx", "gy", None)
    return jax.shard_map(
        shards,
        mesh=mesh,
        in_specs=(place,) * 6,
        out_specs=(place,) * 3,
        check_vma=False,
    )
```

```python
import functools

import jax
import jax.numpy as jnp
from jax import lax
from jax.experimental import pallas as pl
from jax.experimental.pallas import tpu as pltpu
from jax.sharding import PartitionSpec as P

LEVELS = 3
VMEM_LIMIT = (64 * 1024 - 160) * 1024
ROW = 8

FACES = ((1, 0), (-1, 0), (0, 1), (0, -1))
CORNERS = ((1, 1), (1, -1), (-1, 1), (-1, -1))
AROUND = FACES + CORNERS
FAR = ((2, 0), (-2, 0), (0, 2), (0, -2))
WIDE = AROUND + FAR
WIDE_NAMES = ("a", "bx", "by", "bz", "g", "over", "xu", "xl", "yu", "yl", "zu", "zl")
REACH = {1: 4, 2: 3}
ROWS = {1: 16, 2: 8}
WAYS = {1: AROUND, 2: WIDE}


def box(kind, level, way, dims):
    nx, ny, _ = dims
    if level == 2:
        return slice(0, nx), slice(0, ny)
    if kind == "source":
        xs = {0: (0, nx), 1: (1 if way[1] else 0, nx), -1: (0, 3 if way[1] else nx)}[way[0]]
        return slice(*xs), slice(0, ny)
    corner = way[0] != 0 and way[1] != 0
    least = {0: 0, 1: 1 if corner else 0, -1: 0}
    most = {0: 4, 1: 4, -1: 2 if way == (-1, -1) else 3}
    return slice(least[way[0]], most[way[0]]), slice(least[way[1]], most[way[1]])


def layer_shape(dims, way):
    nx, ny, nz = dims
    return (1 if way[0] else nx, 1 if way[1] else ny, nz)


def edge_shape(dims, way):
    return (2, 1, 1, dims[2])


def messages(dims_of):
    found = {}
    for way in FACES:
        found[("first", 0, way)] = layer_shape(dims_of[0], way)
    for level in REACH:
        nx, ny, nz = dims_of[level]
        for way in WAYS[level]:
            found[("raw", level, way)] = (nx, ny, 4, nz)
            found[("source", level, way)] = (nx, ny, nz)
    dims = dims_of[0]
    for way in ((1, 0), (0, 1)):
        found[("lower", 0, way)] = layer_shape(dims, way)
    for way in FACES:
        found[("toward", 0, way)] = layer_shape(dims, way)
        found[("ends", 0, way)] = edge_shape(dims, way)
    for half in range(2):
        for way in AROUND:
            found[("half%d" % half, 0, way)] = layer_shape(dims, way)
    return found


def at_side(dims, way):
    nx, ny, _ = dims
    xs = {0: slice(0, nx), 1: slice(nx - 1, nx), -1: slice(0, 1)}[way[0]]
    ys = {0: slice(0, ny), 1: slice(ny - 1, ny), -1: slice(0, 1)}[way[1]]
    return xs, ys


def halo_place(dims, way):
    nx, ny, _ = dims
    xs = {0: slice(1, 1 + nx), 1: slice(nx + 1, nx + 2), -1: slice(0, 1)}[way[0]]
    ys = {0: slice(ROW, ROW + ny), 1: slice(ROW + ny, ROW + ny + 1), -1: slice(ROW - 1, ROW)}[way[1]]
    return xs, ys


def parity_at(shape, offset=0):
    total = (
        lax.broadcasted_iota(jnp.int32, shape, 0)
        + lax.broadcasted_iota(jnp.int32, shape, 1)
        + lax.broadcasted_iota(jnp.int32, shape, 2)
        + offset
    )
    return (total & 1) == 1


def kernel(dims_of, keys, *refs):
    refs = list(refs)
    args = refs[:6]
    outs = refs[6:9]
    u_in, f_in, a_in, bx_in, by_in, bz_in = held = refs[9:15]
    load_sem, store_sem = refs[15:17]
    kept = refs[17:20]
    refs = refs[20:]
    n_keys = len(keys)
    out_buf = dict(zip(keys, refs[:n_keys]))
    in_buf = dict(zip(keys, refs[n_keys : 2 * n_keys]))
    refs = refs[2 * n_keys :]
    names = ("open", "shut", "g", "diag", "xu", "xl", "yu", "yl", "zu", "zl", "a", "bx", "by", "bz")
    per = [dict(zip(names, refs[:14]))]
    refs = refs[14:]
    for level in REACH:
        per.append(dict(zip(names[-4:], refs[:4])))
        refs = refs[4:]
    pair_t, cols_t = refs[0:2], refs[2:4]
    send_sem, recv_sem = refs[4], refs[5]
    wides = {1: dict(zip(WIDE_NAMES, refs[6:18])), 2: dict(zip(WIDE_NAMES, refs[18:30]))}

    gx, gy = lax.axis_index("gx"), lax.axis_index("gy")
    n_x, n_y = lax.axis_size("gx"), lax.axis_size("gy")

    def inside(dx, dy):
        ok = None
        for place, step, count in ((gx, dx, n_x), (gy, dy, n_y)):
            if step == 0:
                continue
            here = (place + step < count) if step > 0 else (place + step >= 0)
            ok = here if ok is None else jnp.logical_and(ok, here)
        return ok

    def copy_of(key):
        way = key[2]
        index = keys.index(key)
        src, dst = out_buf[key], in_buf[key]
        if key[0] in ("raw", "source"):
            xs, ys = box(*key, dims_of[key[1]])
            src, dst = out_buf[key[:2] + WIDE[:1]].at[xs, ys], dst.at[xs, ys]
        return pltpu.make_async_remote_copy(
            src_ref=src,
            dst_ref=dst,
            send_sem=send_sem.at[index],
            recv_sem=recv_sem.at[index],
            device_id={"gx": gx + way[0], "gy": gy + way[1]},
            device_id_type=pl.DeviceIdType.MESH,
        )

    def send(group):
        for way in WIDE:
            chosen = [key for key in group if key[2] == way]
            if chosen:

                @pl.when(inside(*way))
                def _():
                    for key in chosen:
                        copy_of(key).start()

    def receive(group):
        for way in WIDE:
            chosen = [key for key in group if key[2] == way]
            if chosen:

                @pl.when(inside(-way[0], -way[1]))
                def _():
                    for key in chosen:
                        copy_of(key).wait_recv()

    def group_of(kind, level):
        return [key for key in keys if key[0] == kind and key[1] == level]

    stores = [pltpu.make_async_copy(kept[n], outs[n], store_sem.at[n]) for n in range(LEVELS)]
    loads = [pltpu.make_async_copy(args[n], held[n], load_sem.at[n]) for n in range(6)]

    barrier = pltpu.get_barrier_semaphore()
    for way in WIDE:

        @pl.when(inside(*way))
        def _():
            pl.semaphore_signal(
                barrier,
                inc=1,
                device_id={"gx": gx + way[0], "gy": gy + way[1]},
                device_id_type=pl.DeviceIdType.MESH,
            )

    for n in (0, 3, 4, 2, 5, 1):
        loads[n].start()

    def put_faces(kind, level, source, ways):
        for way in ways:
            xs, ys = at_side(dims_of[level], way)
            out_buf[(kind, level, way)][...] = source[xs, ys, :]

    loads[0].wait()
    put_faces("first", 0, u_in, FACES)

    def put_lower(level):
        for way, name in (((1, 0), "bx"), ((0, 1), "by")):
            xs, ys = at_side(dims_of[level], way)
            out_buf[("lower", level, way)][...] = per[level][name][xs, ys, :]

    loads[3].wait()
    per[0]["bx"][...] = bx_in[...].astype(jnp.float32)
    loads[4].wait()
    per[0]["by"][...] = by_in[...].astype(jnp.float32)
    put_lower(0)

    for way in AROUND:
        chosen = [key for key in keys if key[2] == way and key[0] not in ("raw", "source")]

        @pl.when(jnp.logical_not(inside(-way[0], -way[1])))
        def _():
            for key in chosen:
                in_buf[key][...] = jnp.zeros(in_buf[key].shape, jnp.float32)

    beside_x = (gx > 0).astype(jnp.int32) + (gx + 1 < n_x).astype(jnp.int32)
    beside_y = (gy > 0).astype(jnp.int32) + (gy + 1 < n_y).astype(jnp.int32)
    far_x = (gx > 1).astype(jnp.int32) + (gx + 2 < n_x).astype(jnp.int32)
    far_y = (gy > 1).astype(jnp.int32) + (gy + 2 < n_y).astype(jnp.int32)
    pl.semaphore_wait(barrier, beside_x + beside_y + beside_x * beside_y + far_x + far_y)

    send(group_of("first", 0) + group_of("lower", 0))
    loads[2].wait()
    per[0]["a"][...] = a_in[...].astype(jnp.float32)
    loads[5].wait()
    per[0]["bz"][...] = bz_in[...].astype(jnp.float32)
    loads[1].wait()

    def pair_matrix(size):
        fine = lax.broadcasted_iota(jnp.int32, (size, size // 2), 0)
        coarse = lax.broadcasted_iota(jnp.int32, (size, size // 2), 1)
        return jnp.where((fine >> 1) == coarse, 1.0, 0.0).astype(jnp.bfloat16)

    def three(v):
        high = v.astype(jnp.bfloat16)
        rest = v - high.astype(jnp.float32)
        mid = rest.astype(jnp.bfloat16)
        low = (rest - mid.astype(jnp.float32)).astype(jnp.bfloat16)
        return [high, mid, low]

    def sum_pairs_z(v):
        rows, size = v.shape
        parts = jnp.concatenate(three(v), axis=0)
        got = jnp.dot(parts, pair_matrix(size), preferred_element_type=jnp.float32)
        return got[:rows] + got[rows : 2 * rows] + got[2 * rows :]

    def squeeze(level, sources, ways):
        nx, ny, nz = dims_of[level]
        tmp, cols = pair_t[level], cols_t[level]
        hx, hy = nx // 2, ny // 2
        kept = len(sources)
        odd = (lax.broadcasted_iota(jnp.int32, (1, 1, nz), 2) & 1) == 1
        for n, (source, way) in enumerate(zip(sources, ways)):
            for i in range(hx):
                v = source(2 * i + 1)
                if way != 0:
                    v = source(2 * i) + v
                tmp[n * hx + i : n * hx + i + 1] = v
            some = slice(n * hx, (n + 1) * hx)
            for j in range(hy):
                v = tmp[some, 2 * j + 1 : 2 * j + 2, :]
                if way != 1:
                    v = v + tmp[some, 2 * j : 2 * j + 1, :]
                if way == 2:
                    v = jnp.where(odd, v, 0.0)
                cols[some, j : j + 1, :] = v * (0.125 if way is None else 0.25)
        total = kept * hx
        flat = cols[0:total].reshape(total * 8, nz)
        got = sum_pairs_z(flat).reshape(total, 8, nz // 2)
        return [got[n * hx : (n + 1) * hx, 0:hy, :] for n in range(kept)]

    def coarse_coefs(level):
        these = per[level]
        names = ("a", "bx", "by", "bz")
        sources = [
            functools.partial(lambda ref, i: ref[i : i + 1], these[name]) for name in names
        ]
        for name, v in zip(names, squeeze(level, sources, (None, 0, 1, 2))):
            per[level + 1][name][...] = v

    def make_coefs(level):
        these = per[level]
        nx, ny, nz = dims_of[level]
        scale = 0.25**level
        lower_x = in_buf[("lower", level, (1, 0))]
        lower_y = in_buf[("lower", level, (0, 1))]
        pad = these["open"]
        last = lax.broadcasted_iota(jnp.int32, (nx, ny, nz), 2)
        bx, by, bz = these["bx"][...], these["by"][...], these["bz"][...]
        bxl = jnp.concatenate([lower_x[...], bx[:-1]], axis=0) if nx > 1 else lower_x[...]
        pad[1 : 1 + nx, ROW : ROW + ny, :] = by
        pad[1 : 1 + nx, ROW - 1 : ROW, :] = lower_y[...]
        byl = pad[1 : 1 + nx, ROW - 1 : ROW - 1 + ny, :]
        bzl = jnp.where(last == 0, 0.0, pltpu.roll(bz, 1, 2))
        diag = these["a"][...] + scale * ((bx + bxl) + (by + byl) + (bz + bzl))
        over = 1.0 / diag
        these["diag"][...] = diag
        over_s = over * scale
        these["xu"][...] = bx * over_s
        these["xl"][...] = bxl * over_s
        these["yu"][...] = by * over_s
        these["yl"][...] = byl * over_s
        these["zu"][...] = jnp.where(last == nz - 1, 0.0, bz * over_s)
        these["zl"][...] = bzl * over_s
        return over

    toward_name = {(1, 0): "xu", (-1, 0): "xl", (0, 1): "yu", (0, -1): "yl"}

    def end_ways(way):
        return ((way[0], -1), (way[0], 1)) if way[0] else ((-1, way[1]), (1, way[1]))

    def cross(way, corner):
        return (0, corner[1]) if way[0] else (corner[0], 0)

    def put_toward(level):
        these = per[level]
        dims = dims_of[level]
        nx, ny, nz = dims
        for way in FACES:
            xs, ys = at_side(dims, way)
            shape = layer_shape(dims, way)
            offset = (xs.start + ys.start) & 1
            out_buf[("toward", level, way)][...] = jnp.where(
                parity_at(shape, offset), these[toward_name[way]][xs, ys, :], 0.0
            )
            for n, corner in enumerate(end_ways(way)):
                cxs, cys = at_side(dims, corner)
                offset = (cxs.start + cys.start) & 1
                out_buf[("ends", level, way)][n] = jnp.where(
                    parity_at((1, 1, nz), offset),
                    these[toward_name[cross(way, corner)]][cxs, cys, :],
                    0.0,
                )
        send(group_of("toward", level) + group_of("ends", level))

    def sums(level, pad):
        these = per[level]
        nx, ny, nz = dims_of[level]
        own = pad[1 : 1 + nx, ROW : ROW + ny, :]
        total = these["g"][...]
        total = total + these["xu"][...] * pad[2 : 2 + nx, ROW : ROW + ny, :]
        total = total + these["xl"][...] * pad[0:nx, ROW : ROW + ny, :]
        total = total + these["yu"][...] * pad[1 : 1 + nx, ROW + 1 : ROW + 1 + ny, :]
        total = total + these["yl"][...] * pad[1 : 1 + nx, ROW - 1 : ROW - 1 + ny, :]
        total = total + these["zu"][...] * pltpu.roll(own, nz - 1, 2)
        total = total + these["zl"][...] * pltpu.roll(own, 1, 2)
        return own, total

    def half_sweep(level, half, red):
        these = per[level]
        dims = dims_of[level]
        nx, ny, nz = dims
        shut, pad = these["shut"], these["open"]
        kind = "half%d" % half
        black = parity_at(dims)
        shut[1 : 1 + nx, ROW : ROW + ny, :] = red
        _, total = sums(level, shut)
        value = jnp.where(black, total, red)
        pad[1 : 1 + nx, ROW : ROW + ny, :] = value
        group = group_of(kind, level)
        for key in group:
            xs, ys = at_side(dims, key[2])
            out_buf[key][...] = pad[
                xs.start + 1 : xs.stop + 1, ys.start + ROW : ys.stop + ROW, :
            ]
        send(group)

    def finish_half(level, half, last):
        these = per[level]
        dims = dims_of[level]
        nx, ny, nz = dims
        pad = these["open"]
        kind = "half%d" % half
        group = group_of(kind, level)
        receive(group)
        if half == 0:
            receive(group_of("toward", level) + group_of("ends", level))
        back = lambda way: (-way[0], -way[1])
        if not last:
            for way in FACES:
                xs, ys = at_side(dims, way)
                mine = out_buf[(kind, level, way)][...]
                theirs = in_buf[(kind, level, back(way))][...]
                theirs = theirs + in_buf[("toward", level, back(way))][...] * mine
                hx, hy = halo_place(dims, way)
                pad[hx, hy, :] = theirs
                ends = in_buf[("ends", level, back(way))]
                for n, corner in enumerate(end_ways(way)):
                    cx, cy = at_side(dims, corner)
                    px = hx if way[0] else slice(1 + cx.start, 1 + cx.stop)
                    py = hy if way[1] else slice(ROW + cy.start, ROW + cy.stop)
                    column = in_buf[(kind, level, back(corner))][...]
                    pad[px, py, :] = pad[px, py, :] + ends[n] * column
        for way in FACES:
            xs, ys = at_side(dims, way)
            px = slice(1 + xs.start, 1 + xs.stop)
            py = slice(ROW + ys.start, ROW + ys.stop)
            theirs = in_buf[(kind, level, back(way))][...]
            pad[px, py, :] = pad[px, py, :] + out_buf[("toward", level, way)][...] * theirs

    def put_raw(level):
        buffer = out_buf[("raw", level, WIDE[0])]
        for c, name in enumerate(WIDE_NAMES[:4]):
            for y in range(dims_of[level][1]):
                buffer[:, y, c : c + 1, :] = per[level][name][:, y : y + 1, :]

    def spread(kind, level, ways, targets):
        nx, ny, _ = dims_of[level]
        reach = REACH[level]
        for way in ways:
            key = (kind, level, way)
            at_x, at_y = -nx * way[0], -ny * way[1]
            xs, ys = box(*key, dims_of[level])
            x_from, x_to = max(xs.start, -reach - at_x), min(xs.stop, nx + reach - at_x)
            y_from = max(ys.start, -reach - at_y)
            y_to = min(ys.stop, ny + reach - at_y)
            to = (at_y + y_from) % ROWS[level]
            planes = slice(at_x + x_from + reach, at_x + x_to + reach)

            @pl.when(inside(-way[0], -way[1]))
            def _():
                copy_of(key).wait_recv()
                if len(targets) == 1:
                    targets[0][planes, to : to + y_to - y_from, :] = in_buf[key][
                        x_from:x_to, y_from:y_to, :
                    ]
                else:
                    for c, target in enumerate(targets):
                        for y in range(y_from, y_to):
                            row = to + y - y_from
                            target[planes, row : row + 1, :] = in_buf[key][
                                x_from:x_to, y, c : c + 1, :
                            ]

    def lower_x(v):
        return jnp.concatenate([jnp.zeros_like(v[:1]), v[:-1]], axis=0)

    def wide_start(level):
        nx, ny, _ = dims_of[level]
        wide, reach = wides[level], REACH[level]
        for name in WIDE_NAMES[:5]:
            wide[name][...] = jnp.zeros(wide[name].shape, jnp.float32)
        for name in WIDE_NAMES[:4]:
            wide[name][reach : reach + nx, 0:ny, :] = per[level][name][...]

    def wide_diag(level, xs):
        wide = wides[level]
        scale = 0.25**level
        a, bx, by, bz = (wide[name][xs] for name in WIDE_NAMES[:4])
        place = lax.broadcasted_iota(jnp.int32, a.shape, 2)
        if xs.start > 0:
            bxl = wide["bx"][xs.start - 1 : xs.stop - 1]
        else:
            bxl = lower_x(bx)
        byl = pltpu.roll(by, 1, 1)
        bzl = jnp.where(place == 0, 0.0, pltpu.roll(bz, 1, 2))
        diag = a + scale * ((bx + bxl) + (by + byl) + (bz + bzl))
        over = jnp.where(a > 0.0, 1.0 / jnp.where(a > 0.0, diag, 1.0), 0.0)
        return diag, over, (bx, bxl, by, byl, bz, bzl)

    def wide_coefs(level):
        wide = wides[level]
        nz = dims_of[level][2]
        planes = wide["a"].shape[0]
        _, over, faces = wide_diag(level, slice(0, planes))
        over = over * 0.25**level
        bx, bxl, by, byl, bz, bzl = faces
        place = lax.broadcasted_iota(jnp.int32, bz.shape, 2)
        wide["xu"][...], wide["xl"][...] = bx * over, bxl * over
        wide["yu"][...], wide["yl"][...] = by * over, byl * over
        wide["zu"][...] = jnp.where(place == nz - 1, 0.0, bz * over)
        wide["zl"][...] = bzl * over

    def wide_sums(level, u, xs):
        wide = wides[level]
        nz, rows = dims_of[level][2], ROWS[level]
        own = u[1:-1]
        total = wide["g"][xs] + wide["xu"][xs] * u[2:] + wide["xl"][xs] * u[:-2]
        total = total + wide["yu"][xs] * pltpu.roll(own, rows - 1, 1)
        total = total + wide["yl"][xs] * pltpu.roll(own, 1, 1)
        total = total + wide["zu"][xs] * pltpu.roll(own, nz - 1, 2)
        total = total + wide["zl"][xs] * pltpu.roll(own, 1, 2)
        return own, total

    def wide_send(level, source):
        nx, ny, _ = dims_of[level]
        wide, reach = wides[level], REACH[level]
        own = source * wide["over"][reach : reach + nx, 0:ny, :]
        out_buf[("source", level, WIDE[0])][...] = own
        send(group_of("source", level))
        wide["g"][reach : reach + nx, 0:ny, :] = own

    def wide_smooth(level):
        nx, ny, _ = dims_of[level]
        reach = REACH[level]
        spread("source", level, WAYS[level], [wides[level]["g"]])
        g = wides[level]["g"][...]
        u = jnp.where(parity_at(g.shape, reach), 0.0, g)
        first = reach - 3
        if first == 0:
            edge = jnp.zeros_like(u[:1])
            u = jnp.concatenate([edge, u, edge], axis=0)
        for step in range(3):
            xs = slice(first, nx + 2 * reach - first)
            own, total = wide_sums(level, u, xs)
            black = parity_at(total.shape, reach + first)
            u = jnp.where(black, own, total) if step == 1 else jnp.where(black, total, own)
            first += 1
        return u

    dims = dims_of[0]
    nx, ny, nz = dims
    these = per[0]
    pad = these["open"]
    these["shut"][...] = jnp.zeros(these["shut"].shape, jnp.float32)
    red_cells = jnp.logical_not(parity_at(dims))
    receive(group_of("lower", 0))
    these["g"][...] = f_in[...] * make_coefs(0)
    receive(group_of("first", 0))
    pad[1 : 1 + nx, ROW : ROW + ny, :] = u_in[...]
    for way in FACES:
        hx, hy = halo_place(dims, way)
        pad[hx, hy, :] = in_buf[("first", 0, (-way[0], -way[1]))][...]
    own, total = sums(0, pad)
    half_sweep(0, 0, jnp.where(red_cells, total, own))
    put_toward(0)
    coarse_coefs(0)
    put_raw(1)
    send([key for key in group_of("raw", 1) if key[2] in FACES])
    coarse_coefs(1)
    put_raw(2)
    send(group_of("raw", 2))
    wide_start(1)
    finish_half(0, 0, False)
    own, total = sums(0, pad)
    half_sweep(0, 1, jnp.where(red_cells, total, own))
    send([key for key in group_of("raw", 1) if key[2] in CORNERS])
    spread("raw", 1, FACES, [wides[1][name] for name in WIDE_NAMES[:4]])
    middle = slice(REACH[1], REACH[1] + dims_of[1][0])
    diag, over, _ = wide_diag(1, middle)
    middle_diag = per[1]["bx"]
    middle_diag[...] = diag[:, 0 : dims_of[1][1], :]
    wides[1]["over"][middle] = over
    finish_half(0, 1, False)
    kept[0][...] = pad[1 : 1 + nx, ROW : ROW + ny, :]
    stores[0].start()
    own, total = sums(0, pad)
    these["a"][...] = jnp.where(red_cells, these["diag"][...] * (total - own), 0.0)
    take = functools.partial(lambda ref, i: ref[i : i + 1], these["a"])
    wide_send(1, squeeze(0, [take], (None,))[0])

    spread("raw", 1, CORNERS, [wides[1][name] for name in WIDE_NAMES[:4]])
    wide_coefs(1)
    wide_start(2)
    spread("raw", 2, WAYS[2], [wides[2][name] for name in WIDE_NAMES[:4]])
    _, over, _ = wide_diag(2, slice(0, wides[2]["a"].shape[0]))
    wides[2]["over"][...] = over
    wide_coefs(2)
    u = wide_smooth(1)
    ny = dims_of[1][1]
    kept[1][...] = u[1:-1, 0:ny, :]
    stores[1].start()
    own, total = wide_sums(1, u, middle)
    red_cells = jnp.logical_not(parity_at(dims_of[1]))
    per[1]["a"][...] = jnp.where(
        red_cells, middle_diag[...] * (total[:, 0:ny, :] - own[:, 0:ny, :]), 0.0
    )
    take = functools.partial(lambda ref, i: ref[i : i + 1], per[1]["a"])
    wide_send(2, squeeze(1, [take], (None,))[0])

    def sent(chosen_of):
        for way in WIDE:
            chosen = [key for key in keys if key[2] == way and chosen_of(key)]

            @pl.when(inside(*way))
            def _():
                for key in chosen:
                    copy_of(key).wait_send()

    sent(lambda key: key[:2] != ("source", 2))
    u = wide_smooth(2)
    kept[2][...] = u[1:-1, 0 : dims_of[2][1], :]
    stores[2].start()
    sent(lambda key: key[:2] == ("source", 2))

    for copy in stores:
        copy.wait()


def store(*refs):
    given, outs, held, sem = refs[:3], refs[3:6], refs[6:9], refs[9]
    loads = [pltpu.make_async_copy(given[n], held[n], sem.at[n]) for n in range(3)]
    stores = [pltpu.make_async_copy(held[n], outs[n], sem.at[3 + n]) for n in range(3)]
    for copy in loads:
        copy.start()
    for load, copy in zip(loads, stores):
        load.wait()
        copy.start()
    for copy in stores:
        copy.wait()


def shards(solution, right_side, alpha, beta_x, beta_y, beta_z):
    dims_of = [tuple(size >> level for size in solution.shape) for level in range(LEVELS)]
    found = messages(dims_of)
    keys = list(found)
    buffers = [pltpu.VMEM(found[key], jnp.float32) for key in keys]
    fine = dims_of[0]
    scratch = [pltpu.VMEM(fine, jnp.float32)] * 2 + [pltpu.VMEM(fine, jnp.bfloat16)] * 4
    scratch += [pltpu.SemaphoreType.DMA((6,)), pltpu.SemaphoreType.DMA((LEVELS,))]
    scratch += [pltpu.VMEM(dims, jnp.float32) for dims in dims_of]
    scratch += buffers + buffers
    nx, ny, nz = fine
    scratch += [pltpu.VMEM((nx + 2, 24, nz), jnp.float32)] * 2
    scratch += [pltpu.VMEM(fine, jnp.float32)] * 12
    for level in REACH:
        scratch += [pltpu.VMEM(dims_of[level], jnp.float32)] * 4
    for nx, ny, nz in dims_of[:2]:
        scratch += [pltpu.VMEM((4 * nx // 2, ny, nz), jnp.float32)]
    for nx, ny, nz in dims_of[:2]:
        scratch += [pltpu.VMEM((4 * nx // 2, 8, nz), jnp.float32)]
    scratch += [pltpu.SemaphoreType.DMA((len(keys),))] * 2
    for level, reach in REACH.items():
        nx, _, nz = dims_of[level]
        scratch += [pltpu.VMEM((nx + 2 * reach, ROWS[level], nz), jnp.float32)] * 12
    iterates = pl.pallas_call(
        functools.partial(kernel, dims_of, keys),
        out_shape=[jax.ShapeDtypeStruct(dims, jnp.float32) for dims in dims_of],
        in_specs=[pl.BlockSpec(memory_space=pltpu.HBM)] * 6,
        out_specs=[pl.BlockSpec(memory_space=pltpu.HBM)] * 3,
        scratch_shapes=scratch,
        compiler_params=pltpu.CompilerParams(
            collective_id=0, has_side_effects=True, vmem_limit_bytes=VMEM_LIMIT
        ),
        name="vcycle",
    )(solution, right_side, alpha, beta_x, beta_y, beta_z)
    return pl.pallas_call(
        store,
        out_shape=[jax.ShapeDtypeStruct(dims, jnp.float32) for dims in dims_of],
        in_specs=[pl.BlockSpec(memory_space=pltpu.HBM)] * 3,
        out_specs=[pl.BlockSpec(memory_space=pltpu.HBM)] * 3,
        scratch_shapes=[pltpu.VMEM(dims, jnp.float32) for dims in dims_of]
        + [pltpu.SemaphoreType.DMA((6,))],
        compiler_params=pltpu.CompilerParams(vmem_limit_bytes=VMEM_LIMIT),
        name="store",
    )(*iterates)


def solution(mesh):
    place = P("gx", "gy", None)
    return jax.shard_map(
        shards,
        mesh=mesh,
        in_specs=(place,) * 6,
        out_specs=(place,) * 3,
        check_vma=False,
    )
```

```python
import functools

import jax
import jax.numpy as jnp
from jax import lax
from jax.experimental import pallas as pl
from jax.experimental.pallas import tpu as pltpu
from jax.sharding import PartitionSpec as P

LEVELS = 3
VMEM_LIMIT = (64 * 1024 - 160) * 1024
ROW = 8

FACES = ((0, 1), (0, -1), (1, 0), (-1, 0))
CORNERS = ((1, 1), (1, -1), (-1, 1), (-1, -1))
AROUND = FACES + CORNERS
FAR = ((2, 0), (-2, 0), (0, 2), (0, -2))
WIDE = AROUND + FAR
WIDE_NAMES = ("a", "bx", "by", "bz", "g", "over", "xu", "xl", "yu", "yl", "zu", "zl")
REACH = {1: 4, 2: 3}
ROWS = {1: 16, 2: 8}
WAYS = {1: AROUND, 2: WIDE}


def box(kind, level, way, dims):
    nx, ny, _ = dims
    if level == 2:
        return slice(0, nx), slice(0, ny)
    if kind == "source":
        xs = {0: (0, nx), 1: (1 if way[1] else 0, nx), -1: (0, 3 if way[1] else nx)}[way[0]]
        return slice(*xs), slice(0, ny)
    corner = way[0] != 0 and way[1] != 0
    least = {0: 0, 1: 1 if corner else 0, -1: 0}
    most = {0: 4, 1: 4, -1: 2 if way == (-1, -1) else 3}
    return slice(least[way[0]], most[way[0]]), slice(least[way[1]], most[way[1]])


def layer_shape(dims, way):
    nx, ny, nz = dims
    return (1 if way[0] else nx, 1 if way[1] else ny, nz)


def edge_shape(dims, way):
    return (2, 1, 1, dims[2])


def messages(dims_of):
    found = {}
    for way in FACES:
        found[("first", 0, way)] = layer_shape(dims_of[0], way)
    for level in REACH:
        nx, ny, nz = dims_of[level]
        for way in WAYS[level]:
            found[("raw", level, way)] = (nx, ny, 4, nz)
            found[("source", level, way)] = (nx, ny, nz)
    dims = dims_of[0]
    for way in ((1, 0), (0, 1)):
        found[("lower", 0, way)] = layer_shape(dims, way)
    for way in FACES:
        found[("toward", 0, way)] = layer_shape(dims, way)
        found[("ends", 0, way)] = edge_shape(dims, way)
    for half in range(2):
        for way in AROUND:
            found[("half%d" % half, 0, way)] = layer_shape(dims, way)
    return found


def at_side(dims, way):
    nx, ny, _ = dims
    xs = {0: slice(0, nx), 1: slice(nx - 1, nx), -1: slice(0, 1)}[way[0]]
    ys = {0: slice(0, ny), 1: slice(ny - 1, ny), -1: slice(0, 1)}[way[1]]
    return xs, ys


def halo_place(dims, way):
    nx, ny, _ = dims
    xs = {0: slice(1, 1 + nx), 1: slice(nx + 1, nx + 2), -1: slice(0, 1)}[way[0]]
    ys = {0: slice(ROW, ROW + ny), 1: slice(ROW + ny, ROW + ny + 1), -1: slice(ROW - 1, ROW)}[way[1]]
    return xs, ys


def parity_at(shape, offset=0):
    total = (
        lax.broadcasted_iota(jnp.int32, shape, 0)
        + lax.broadcasted_iota(jnp.int32, shape, 1)
        + lax.broadcasted_iota(jnp.int32, shape, 2)
        + offset
    )
    return (total & 1) == 1


def kernel(dims_of, keys, *refs):
    refs = list(refs)
    args = refs[:6]
    outs = refs[6:9]
    u_in, f_in, a_in, bx_in, by_in, bz_in = held = refs[9:15]
    load_sem, store_sem = refs[15:17]
    kept = refs[17:20]
    refs = refs[20:]
    n_keys = len(keys)
    out_buf = dict(zip(keys, refs[:n_keys]))
    in_buf = dict(zip(keys, refs[n_keys : 2 * n_keys]))
    refs = refs[2 * n_keys :]
    names = ("open", "shut", "g", "diag", "xu", "xl", "yu", "yl", "zu", "zl", "a", "bx", "by", "bz")
    per = [dict(zip(names, refs[:14]))]
    refs = refs[14:]
    for level in REACH:
        per.append(dict(zip(names[-4:], refs[:4])))
        refs = refs[4:]
    pair_t, cols_t = refs[0:2], refs[2:4]
    send_sem, recv_sem = refs[4], refs[5]
    wides = {1: dict(zip(WIDE_NAMES, refs[6:18])), 2: dict(zip(WIDE_NAMES, refs[18:30]))}
    pairs = refs[30]

    gx, gy = lax.axis_index("gx"), lax.axis_index("gy")
    n_x, n_y = lax.axis_size("gx"), lax.axis_size("gy")

    def inside(dx, dy):
        ok = None
        for place, step, count in ((gx, dx, n_x), (gy, dy, n_y)):
            if step == 0:
                continue
            here = (place + step < count) if step > 0 else (place + step >= 0)
            ok = here if ok is None else jnp.logical_and(ok, here)
        return ok

    def copy_of(key):
        way = key[2]
        index = keys.index(key)
        src, dst = out_buf[key], in_buf[key]
        if key[0] in ("raw", "source"):
            xs, ys = box(*key, dims_of[key[1]])
            src, dst = out_buf[key[:2] + WIDE[:1]].at[xs, ys], dst.at[xs, ys]
        return pltpu.make_async_remote_copy(
            src_ref=src,
            dst_ref=dst,
            send_sem=send_sem.at[index],
            recv_sem=recv_sem.at[index],
            device_id={"gx": gx + way[0], "gy": gy + way[1]},
            device_id_type=pl.DeviceIdType.MESH,
        )

    def send(group):
        for way in WIDE:
            chosen = [key for key in group if key[2] == way]
            if chosen:

                @pl.when(inside(*way))
                def _():
                    for key in chosen:
                        copy_of(key).start()

    def receive(group):
        for way in WIDE:
            chosen = [key for key in group if key[2] == way]
            if chosen:

                @pl.when(inside(-way[0], -way[1]))
                def _():
                    for key in chosen:
                        copy_of(key).wait_recv()

    def group_of(kind, level):
        return [key for key in keys if key[0] == kind and key[1] == level]

    stores = [pltpu.make_async_copy(kept[n], outs[n], store_sem.at[n]) for n in range(LEVELS)]
    loads = [pltpu.make_async_copy(args[n], held[n], load_sem.at[n]) for n in range(6)]

    barrier = pltpu.get_barrier_semaphore()
    for way in WIDE:

        @pl.when(inside(*way))
        def _():
            pl.semaphore_signal(
                barrier,
                inc=1,
                device_id={"gx": gx + way[0], "gy": gy + way[1]},
                device_id_type=pl.DeviceIdType.MESH,
            )

    for n in (0, 3, 4, 2, 5, 1):
        loads[n].start()

    def put_faces(kind, level, source, ways):
        for way in ways:
            xs, ys = at_side(dims_of[level], way)
            out_buf[(kind, level, way)][...] = source[xs, ys, :]

    size = pairs.shape[0]
    row = lax.broadcasted_iota(jnp.int32, (size, size // 2), 0)
    column = lax.broadcasted_iota(jnp.int32, (size, size // 2), 1)
    pairs[...] = jnp.where((row >> 1) == column, 1.0, 0.0).astype(jnp.bfloat16)
    for level in REACH:
        for name in WIDE_NAMES[:5]:
            wides[level][name][...] = jnp.zeros(wides[level][name].shape, jnp.float32)
    per[0]["shut"][...] = jnp.zeros(per[0]["shut"].shape, jnp.float32)

    loads[0].wait()
    put_faces("first", 0, u_in, FACES)

    def put_lower(level):
        for way, name in (((1, 0), "bx"), ((0, 1), "by")):
            xs, ys = at_side(dims_of[level], way)
            out_buf[("lower", level, way)][...] = per[level][name][xs, ys, :]

    loads[3].wait()
    per[0]["bx"][...] = bx_in[...].astype(jnp.float32)
    loads[4].wait()
    per[0]["by"][...] = by_in[...].astype(jnp.float32)
    put_lower(0)

    for way in AROUND:
        chosen = [key for key in keys if key[2] == way and key[0] not in ("raw", "source")]

        @pl.when(jnp.logical_not(inside(-way[0], -way[1])))
        def _():
            for key in chosen:
                in_buf[key][...] = jnp.zeros(in_buf[key].shape, jnp.float32)

    beside_x = (gx > 0).astype(jnp.int32) + (gx + 1 < n_x).astype(jnp.int32)
    beside_y = (gy > 0).astype(jnp.int32) + (gy + 1 < n_y).astype(jnp.int32)
    far_x = (gx > 1).astype(jnp.int32) + (gx + 2 < n_x).astype(jnp.int32)
    far_y = (gy > 1).astype(jnp.int32) + (gy + 2 < n_y).astype(jnp.int32)
    pl.semaphore_wait(barrier, beside_x + beside_y + beside_x * beside_y + far_x + far_y)

    send(group_of("first", 0) + group_of("lower", 0))
    loads[2].wait()
    per[0]["a"][...] = a_in[...].astype(jnp.float32)
    loads[5].wait()
    per[0]["bz"][...] = bz_in[...].astype(jnp.float32)
    loads[1].wait()

    def three(v):
        high = v.astype(jnp.bfloat16)
        rest = v - high.astype(jnp.float32)
        mid = rest.astype(jnp.bfloat16)
        low = (rest - mid.astype(jnp.float32)).astype(jnp.bfloat16)
        return [high, mid, low]

    def sum_pairs_z(v):
        rows, size = v.shape
        parts = jnp.concatenate(three(v), axis=0)
        got = jnp.dot(parts, pairs[0:size, 0 : size // 2], preferred_element_type=jnp.float32)
        return got[:rows] + got[rows : 2 * rows] + got[2 * rows :]

    def squeeze(level, sources, ways):
        nx, ny, nz = dims_of[level]
        tmp, cols = pair_t[level], cols_t[level]
        hx, hy = nx // 2, ny // 2
        kept = len(sources)
        odd = (lax.broadcasted_iota(jnp.int32, (1, 1, nz), 2) & 1) == 1
        for n, (source, way) in enumerate(zip(sources, ways)):
            for i in range(hx):
                v = source(2 * i + 1)
                if way != 0:
                    v = source(2 * i) + v
                tmp[n * hx + i : n * hx + i + 1] = v
            some = slice(n * hx, (n + 1) * hx)
            for j in range(hy):
                v = tmp[some, 2 * j + 1 : 2 * j + 2, :]
                if way != 1:
                    v = v + tmp[some, 2 * j : 2 * j + 1, :]
                if way == 2:
                    v = jnp.where(odd, v, 0.0)
                cols[some, j : j + 1, :] = v * (0.125 if way is None else 0.25)
        total = kept * hx
        flat = cols[0:total].reshape(total * 8, nz)
        got = sum_pairs_z(flat).reshape(total, 8, nz // 2)
        return [got[n * hx : (n + 1) * hx, 0:hy, :] for n in range(kept)]

    def coarse_coefs(level):
        these = per[level]
        names = ("a", "bx", "by", "bz")
        sources = [
            functools.partial(lambda ref, i: ref[i : i + 1], these[name]) for name in names
        ]
        for name, v in zip(names, squeeze(level, sources, (None, 0, 1, 2))):
            per[level + 1][name][...] = v

    def make_coefs(level):
        these = per[level]
        nx, ny, nz = dims_of[level]
        scale = 0.25**level
        lower_x = in_buf[("lower", level, (1, 0))]
        lower_y = in_buf[("lower", level, (0, 1))]
        pad = these["open"]
        last = lax.broadcasted_iota(jnp.int32, (nx, ny, nz), 2)
        bx, by, bz = these["bx"][...], these["by"][...], these["bz"][...]
        bxl = jnp.concatenate([lower_x[...], bx[:-1]], axis=0) if nx > 1 else lower_x[...]
        pad[1 : 1 + nx, ROW : ROW + ny, :] = by
        pad[1 : 1 + nx, ROW - 1 : ROW, :] = lower_y[...]
        byl = pad[1 : 1 + nx, ROW - 1 : ROW - 1 + ny, :]
        bzl = jnp.where(last == 0, 0.0, pltpu.roll(bz, 1, 2))
        diag = these["a"][...] + scale * ((bx + bxl) + (by + byl) + (bz + bzl))
        over = 1.0 / diag
        these["diag"][...] = diag
        over_s = over * scale
        these["xu"][...] = bx * over_s
        these["xl"][...] = bxl * over_s
        these["yu"][...] = by * over_s
        these["yl"][...] = byl * over_s
        these["zu"][...] = jnp.where(last == nz - 1, 0.0, bz * over_s)
        these["zl"][...] = bzl * over_s
        return over

    toward_name = {(1, 0): "xu", (-1, 0): "xl", (0, 1): "yu", (0, -1): "yl"}

    def end_ways(way):
        return ((way[0], -1), (way[0], 1)) if way[0] else ((-1, way[1]), (1, way[1]))

    def cross(way, corner):
        return (0, corner[1]) if way[0] else (corner[0], 0)

    def put_toward(level):
        these = per[level]
        dims = dims_of[level]
        nx, ny, nz = dims
        for way in FACES:
            xs, ys = at_side(dims, way)
            shape = layer_shape(dims, way)
            offset = (xs.start + ys.start) & 1
            out_buf[("toward", level, way)][...] = jnp.where(
                parity_at(shape, offset), these[toward_name[way]][xs, ys, :], 0.0
            )
            for n, corner in enumerate(end_ways(way)):
                cxs, cys = at_side(dims, corner)
                offset = (cxs.start + cys.start) & 1
                out_buf[("ends", level, way)][n] = jnp.where(
                    parity_at((1, 1, nz), offset),
                    these[toward_name[cross(way, corner)]][cxs, cys, :],
                    0.0,
                )
        send(group_of("toward", level) + group_of("ends", level))

    def sums(level, pad):
        these = per[level]
        nx, ny, nz = dims_of[level]
        own = pad[1 : 1 + nx, ROW : ROW + ny, :]
        total = these["g"][...]
        total = total + these["xu"][...] * pad[2 : 2 + nx, ROW : ROW + ny, :]
        total = total + these["xl"][...] * pad[0:nx, ROW : ROW + ny, :]
        total = total + these["yu"][...] * pad[1 : 1 + nx, ROW + 1 : ROW + 1 + ny, :]
        total = total + these["yl"][...] * pad[1 : 1 + nx, ROW - 1 : ROW - 1 + ny, :]
        total = total + these["zu"][...] * pltpu.roll(own, nz - 1, 2)
        total = total + these["zl"][...] * pltpu.roll(own, 1, 2)
        return own, total

    def half_sweep(level, half, red):
        these = per[level]
        dims = dims_of[level]
        nx, ny, nz = dims
        shut, pad = these["shut"], these["open"]
        kind = "half%d" % half
        black = parity_at(dims)
        shut[1 : 1 + nx, ROW : ROW + ny, :] = red
        _, total = sums(level, shut)
        value = jnp.where(black, total, red)
        pad[1 : 1 + nx, ROW : ROW + ny, :] = value
        group = group_of(kind, level)
        for key in group:
            xs, ys = at_side(dims, key[2])
            out_buf[key][...] = pad[
                xs.start + 1 : xs.stop + 1, ys.start + ROW : ys.stop + ROW, :
            ]
        send(group)

    def finish_half(level, half, last):
        these = per[level]
        dims = dims_of[level]
        nx, ny, nz = dims
        pad = these["open"]
        kind = "half%d" % half
        group = group_of(kind, level)
        receive(group)
        if half == 0:
            receive(group_of("toward", level) + group_of("ends", level))
        back = lambda way: (-way[0], -way[1])
        if not last:
            for way in FACES:
                xs, ys = at_side(dims, way)
                mine = out_buf[(kind, level, way)][...]
                theirs = in_buf[(kind, level, back(way))][...]
                theirs = theirs + in_buf[("toward", level, back(way))][...] * mine
                hx, hy = halo_place(dims, way)
                pad[hx, hy, :] = theirs
                ends = in_buf[("ends", level, back(way))]
                for n, corner in enumerate(end_ways(way)):
                    cx, cy = at_side(dims, corner)
                    px = hx if way[0] else slice(1 + cx.start, 1 + cx.stop)
                    py = hy if way[1] else slice(ROW + cy.start, ROW + cy.stop)
                    column = in_buf[(kind, level, back(corner))][...]
                    pad[px, py, :] = pad[px, py, :] + ends[n] * column
        for way in FACES:
            xs, ys = at_side(dims, way)
            px = slice(1 + xs.start, 1 + xs.stop)
            py = slice(ROW + ys.start, ROW + ys.stop)
            theirs = in_buf[(kind, level, back(way))][...]
            pad[px, py, :] = pad[px, py, :] + out_buf[("toward", level, way)][...] * theirs

    def put_raw(level):
        buffer = out_buf[("raw", level, WIDE[0])]
        for c, name in enumerate(WIDE_NAMES[:4]):
            for y in range(dims_of[level][1]):
                buffer[:, y, c : c + 1, :] = per[level][name][:, y : y + 1, :]

    def spread(kind, level, ways, targets):
        nx, ny, _ = dims_of[level]
        reach = REACH[level]
        for way in ways:
            key = (kind, level, way)
            at_x, at_y = -nx * way[0], -ny * way[1]
            xs, ys = box(*key, dims_of[level])
            x_from, x_to = max(xs.start, -reach - at_x), min(xs.stop, nx + reach - at_x)
            y_from = max(ys.start, -reach - at_y)
            y_to = min(ys.stop, ny + reach - at_y)
            to = (at_y + y_from) % ROWS[level]
            planes = slice(at_x + x_from + reach, at_x + x_to + reach)

            @pl.when(inside(-way[0], -way[1]))
            def _():
                copy_of(key).wait_recv()
                if len(targets) == 1:
                    targets[0][planes, to : to + y_to - y_from, :] = in_buf[key][
                        x_from:x_to, y_from:y_to, :
                    ]
                else:
                    for c, target in enumerate(targets):
                        for y in range(y_from, y_to):
                            row = to + y - y_from
                            target[planes, row : row + 1, :] = in_buf[key][
                                x_from:x_to, y, c : c + 1, :
                            ]

    def lower_x(v):
        return jnp.concatenate([jnp.zeros_like(v[:1]), v[:-1]], axis=0)

    def wide_start(level):
        nx, ny, _ = dims_of[level]
        wide, reach = wides[level], REACH[level]
        for name in WIDE_NAMES[:4]:
            wide[name][reach : reach + nx, 0:ny, :] = per[level][name][...]

    def wide_diag(level, xs):
        wide = wides[level]
        scale = 0.25**level
        a, bx, by, bz = (wide[name][xs] for name in WIDE_NAMES[:4])
        place = lax.broadcasted_iota(jnp.int32, a.shape, 2)
        if xs.start > 0:
            bxl = wide["bx"][xs.start - 1 : xs.stop - 1]
        else:
            bxl = lower_x(bx)
        byl = pltpu.roll(by, 1, 1)
        bzl = jnp.where(place == 0, 0.0, pltpu.roll(bz, 1, 2))
        diag = a + scale * ((bx + bxl) + (by + byl) + (bz + bzl))
        over = jnp.where(a > 0.0, 1.0 / jnp.where(a > 0.0, diag, 1.0), 0.0)
        return diag, over, (bx, bxl, by, byl, bz, bzl)

    def wide_coefs(level):
        wide = wides[level]
        nz = dims_of[level][2]
        planes = wide["a"].shape[0]
        _, over, faces = wide_diag(level, slice(0, planes))
        over = over * 0.25**level
        bx, bxl, by, byl, bz, bzl = faces
        place = lax.broadcasted_iota(jnp.int32, bz.shape, 2)
        wide["xu"][...], wide["xl"][...] = bx * over, bxl * over
        wide["yu"][...], wide["yl"][...] = by * over, byl * over
        wide["zu"][...] = jnp.where(place == nz - 1, 0.0, bz * over)
        wide["zl"][...] = bzl * over

    def wide_sums(level, u, xs):
        wide = wides[level]
        nz, rows = dims_of[level][2], ROWS[level]
        own = u[1:-1]
        total = wide["g"][xs] + wide["xu"][xs] * u[2:] + wide["xl"][xs] * u[:-2]
        total = total + wide["yu"][xs] * pltpu.roll(own, rows - 1, 1)
        total = total + wide["yl"][xs] * pltpu.roll(own, 1, 1)
        total = total + wide["zu"][xs] * pltpu.roll(own, nz - 1, 2)
        total = total + wide["zl"][xs] * pltpu.roll(own, 1, 2)
        return own, total

    def wide_send(level, source):
        nx, ny, _ = dims_of[level]
        wide, reach = wides[level], REACH[level]
        own = source * wide["over"][reach : reach + nx, 0:ny, :]
        out_buf[("source", level, WIDE[0])][...] = own
        send(group_of("source", level))
        wide["g"][reach : reach + nx, 0:ny, :] = own

    def wide_smooth(level):
        nx, ny, _ = dims_of[level]
        reach = REACH[level]
        spread("source", level, WAYS[level], [wides[level]["g"]])
        g = wides[level]["g"][...]
        u = jnp.where(parity_at(g.shape, reach), 0.0, g)
        first = reach - 3
        if first == 0:
            edge = jnp.zeros_like(u[:1])
            u = jnp.concatenate([edge, u, edge], axis=0)
        for step in range(3):
            xs = slice(first, nx + 2 * reach - first)
            own, total = wide_sums(level, u, xs)
            black = parity_at(total.shape, reach + first)
            u = jnp.where(black, own, total) if step == 1 else jnp.where(black, total, own)
            first += 1
        return u

    dims = dims_of[0]
    nx, ny, nz = dims
    these = per[0]
    pad = these["open"]
    red_cells = jnp.logical_not(parity_at(dims))
    coarse_coefs(0)
    put_raw(1)
    wide_start(1)
    receive(group_of("lower", 0))
    these["g"][...] = f_in[...] * make_coefs(0)
    receive(group_of("first", 0))
    pad[1 : 1 + nx, ROW : ROW + ny, :] = u_in[...]
    for way in FACES:
        hx, hy = halo_place(dims, way)
        pad[hx, hy, :] = in_buf[("first", 0, (-way[0], -way[1]))][...]
    own, total = sums(0, pad)
    half_sweep(0, 0, jnp.where(red_cells, total, own))
    put_toward(0)
    send([key for key in group_of("raw", 1) if key[2] in FACES])
    coarse_coefs(1)
    put_raw(2)
    send(group_of("raw", 2))
    wide_start(2)
    finish_half(0, 0, False)
    own, total = sums(0, pad)
    half_sweep(0, 1, jnp.where(red_cells, total, own))
    send([key for key in group_of("raw", 1) if key[2] in CORNERS])
    spread("raw", 1, FACES, [wides[1][name] for name in WIDE_NAMES[:4]])
    middle = slice(REACH[1], REACH[1] + dims_of[1][0])
    diag, over, _ = wide_diag(1, middle)
    middle_diag = per[1]["bx"]
    middle_diag[...] = diag[:, 0 : dims_of[1][1], :]
    wides[1]["over"][middle] = over
    spread("raw", 2, WAYS[2], [wides[2][name] for name in WIDE_NAMES[:4]])
    _, over, _ = wide_diag(2, slice(0, wides[2]["a"].shape[0]))
    wides[2]["over"][...] = over
    wide_coefs(2)
    finish_half(0, 1, False)
    kept[0][...] = pad[1 : 1 + nx, ROW : ROW + ny, :]
    stores[0].start()
    own, total = sums(0, pad)
    these["a"][...] = jnp.where(red_cells, these["diag"][...] * (total - own), 0.0)
    take = functools.partial(lambda ref, i: ref[i : i + 1], these["a"])
    wide_send(1, squeeze(0, [take], (None,))[0])

    spread("raw", 1, CORNERS, [wides[1][name] for name in WIDE_NAMES[:4]])
    wide_coefs(1)
    u = wide_smooth(1)
    ny = dims_of[1][1]
    kept[1][...] = u[1:-1, 0:ny, :]
    stores[1].start()
    own, total = wide_sums(1, u, middle)
    red_cells = jnp.logical_not(parity_at(dims_of[1]))
    per[1]["a"][...] = jnp.where(
        red_cells, middle_diag[...] * (total[:, 0:ny, :] - own[:, 0:ny, :]), 0.0
    )
    take = functools.partial(lambda ref, i: ref[i : i + 1], per[1]["a"])
    wide_send(2, squeeze(1, [take], (None,))[0])

    def sent(chosen_of):
        for way in WIDE:
            chosen = [key for key in keys if key[2] == way and chosen_of(key)]

            @pl.when(inside(*way))
            def _():
                for key in chosen:
                    copy_of(key).wait_send()

    sent(lambda key: key[:2] != ("source", 2))
    u = wide_smooth(2)
    kept[2][...] = u[1:-1, 0 : dims_of[2][1], :]
    stores[2].start()
    sent(lambda key: key[:2] == ("source", 2))

    for copy in stores:
        copy.wait()


def store(*refs):
    given, outs, held, sem = refs[:3], refs[3:6], refs[6:9], refs[9]
    loads = [pltpu.make_async_copy(given[n], held[n], sem.at[n]) for n in range(3)]
    stores = [pltpu.make_async_copy(held[n], outs[n], sem.at[3 + n]) for n in range(3)]
    for copy in loads:
        copy.start()
    for load, copy in zip(loads, stores):
        load.wait()
        copy.start()
    for copy in stores:
        copy.wait()


def shards(solution, right_side, alpha, beta_x, beta_y, beta_z):
    dims_of = [tuple(size >> level for size in solution.shape) for level in range(LEVELS)]
    found = messages(dims_of)
    keys = list(found)
    buffers = [pltpu.VMEM(found[key], jnp.float32) for key in keys]
    fine = dims_of[0]
    scratch = [pltpu.VMEM(fine, jnp.float32)] * 2 + [pltpu.VMEM(fine, jnp.bfloat16)] * 4
    scratch += [pltpu.SemaphoreType.DMA((6,)), pltpu.SemaphoreType.DMA((LEVELS,))]
    scratch += [pltpu.VMEM(dims, jnp.float32) for dims in dims_of]
    scratch += buffers + buffers
    nx, ny, nz = fine
    scratch += [pltpu.VMEM((nx + 2, 24, nz), jnp.float32)] * 2
    scratch += [pltpu.VMEM(fine, jnp.float32)] * 12
    for level in REACH:
        scratch += [pltpu.VMEM(dims_of[level], jnp.float32)] * 4
    for nx, ny, nz in dims_of[:2]:
        scratch += [pltpu.VMEM((4 * nx // 2, ny, nz), jnp.float32)]
    for nx, ny, nz in dims_of[:2]:
        scratch += [pltpu.VMEM((4 * nx // 2, 8, nz), jnp.float32)]
    scratch += [pltpu.SemaphoreType.DMA((len(keys),))] * 2
    for level, reach in REACH.items():
        nx, _, nz = dims_of[level]
        scratch += [pltpu.VMEM((nx + 2 * reach, ROWS[level], nz), jnp.float32)] * 12
    scratch += [pltpu.VMEM((fine[2], fine[2] // 2), jnp.bfloat16)]
    iterates = pl.pallas_call(
        functools.partial(kernel, dims_of, keys),
        out_shape=[jax.ShapeDtypeStruct(dims, jnp.float32) for dims in dims_of],
        in_specs=[pl.BlockSpec(memory_space=pltpu.HBM)] * 6,
        out_specs=[pl.BlockSpec(memory_space=pltpu.HBM)] * 3,
        scratch_shapes=scratch,
        compiler_params=pltpu.CompilerParams(
            collective_id=0, has_side_effects=True, vmem_limit_bytes=VMEM_LIMIT
        ),
        name="vcycle",
    )(solution, right_side, alpha, beta_x, beta_y, beta_z)
    return pl.pallas_call(
        store,
        out_shape=[jax.ShapeDtypeStruct(dims, jnp.float32) for dims in dims_of],
        in_specs=[pl.BlockSpec(memory_space=pltpu.HBM)] * 3,
        out_specs=[pl.BlockSpec(memory_space=pltpu.HBM)] * 3,
        scratch_shapes=[pltpu.VMEM(dims, jnp.float32) for dims in dims_of]
        + [pltpu.SemaphoreType.DMA((6,))],
        compiler_params=pltpu.CompilerParams(vmem_limit_bytes=VMEM_LIMIT),
        name="store",
    )(*iterates)


def solution(mesh):
    place = P("gx", "gy", None)
    return jax.shard_map(
        shards,
        mesh=mesh,
        in_specs=(place,) * 6,
        out_specs=(place,) * 3,
        check_vma=False,
    )
```

```python
import functools

import jax
import jax.numpy as jnp
from jax import lax
from jax.experimental import pallas as pl
from jax.experimental.pallas import tpu as pltpu
from jax.sharding import PartitionSpec as P

LEVELS = 3
VMEM_LIMIT = (64 * 1024 - 160) * 1024
ROW = 8

FACES = ((0, 1), (0, -1), (1, 0), (-1, 0))
CORNERS = ((1, 1), (1, -1), (-1, 1), (-1, -1))
AROUND = FACES + CORNERS
FAR = ((2, 0), (-2, 0), (0, 2), (0, -2))
WIDE = AROUND + FAR
WIDE_NAMES = ("a", "bx", "by", "bz", "g", "over", "xu", "xl", "yu", "yl", "zu", "zl")
REACH = {1: 4, 2: 3}
ROWS = {1: 16, 2: 8}
WAYS = {1: AROUND, 2: WIDE}


def box(kind, level, way, dims):
    nx, ny, _ = dims
    if level == 2:
        return slice(0, nx), slice(0, ny)
    if kind == "source":
        xs = {0: (0, nx), 1: (1 if way[1] else 0, nx), -1: (0, 3 if way[1] else nx)}[way[0]]
        return slice(*xs), slice(0, ny)
    corner = way[0] != 0 and way[1] != 0
    least = {0: 0, 1: 1 if corner else 0, -1: 0}
    most = {0: 4, 1: 4, -1: 2 if way == (-1, -1) else 3}
    return slice(least[way[0]], most[way[0]]), slice(least[way[1]], most[way[1]])


def layer_shape(dims, way):
    nx, ny, nz = dims
    return (1 if way[0] else nx, 1 if way[1] else ny, nz)


def edge_shape(dims, way):
    return (2, 1, 1, dims[2])


def messages(dims_of):
    found = {}
    for way in FACES:
        found[("first", 0, way)] = layer_shape(dims_of[0], way)
    for level in REACH:
        nx, ny, nz = dims_of[level]
        for way in WAYS[level]:
            found[("raw", level, way)] = (nx, ny, 4, nz)
            found[("source", level, way)] = (nx, ny, nz)
    dims = dims_of[0]
    for way in ((1, 0), (0, 1)):
        found[("lower", 0, way)] = layer_shape(dims, way)
    for way in FACES:
        found[("toward", 0, way)] = layer_shape(dims, way)
        found[("ends", 0, way)] = edge_shape(dims, way)
    for half in range(2):
        for way in AROUND:
            found[("half%d" % half, 0, way)] = layer_shape(dims, way)
    return found


def at_side(dims, way):
    nx, ny, _ = dims
    xs = {0: slice(0, nx), 1: slice(nx - 1, nx), -1: slice(0, 1)}[way[0]]
    ys = {0: slice(0, ny), 1: slice(ny - 1, ny), -1: slice(0, 1)}[way[1]]
    return xs, ys


def halo_place(dims, way):
    nx, ny, _ = dims
    xs = {0: slice(1, 1 + nx), 1: slice(nx + 1, nx + 2), -1: slice(0, 1)}[way[0]]
    ys = {0: slice(ROW, ROW + ny), 1: slice(ROW + ny, ROW + ny + 1), -1: slice(ROW - 1, ROW)}[way[1]]
    return xs, ys


def parity_at(shape, offset=0):
    total = (
        lax.broadcasted_iota(jnp.int32, shape, 0)
        + lax.broadcasted_iota(jnp.int32, shape, 1)
        + lax.broadcasted_iota(jnp.int32, shape, 2)
        + offset
    )
    return (total & 1) == 1


def kernel(dims_of, keys, *refs):
    refs = list(refs)
    args = refs[:6]
    outs = refs[6:9]
    u_in, f_in, a_in, bx_in, by_in, bz_in = held = refs[9:15]
    load_sem, store_sem = refs[15:17]
    kept = refs[17:20]
    refs = refs[20:]
    n_keys = len(keys)
    out_buf = dict(zip(keys, refs[:n_keys]))
    in_buf = dict(zip(keys, refs[n_keys : 2 * n_keys]))
    refs = refs[2 * n_keys :]
    names = ("open", "shut", "g", "diag", "xu", "xl", "yu", "yl", "zu", "zl", "a", "bx", "by", "bz")
    per = [dict(zip(names, refs[:14]))]
    refs = refs[14:]
    for level in REACH:
        per.append(dict(zip(names[-4:], refs[:4])))
        refs = refs[4:]
    pair_t, cols_t = refs[0:2], refs[2:4]
    send_sem, recv_sem = refs[4], refs[5]
    wides = {1: dict(zip(WIDE_NAMES, refs[6:18])), 2: dict(zip(WIDE_NAMES, refs[18:30]))}
    pairs = refs[30]

    gx, gy = lax.axis_index("gx"), lax.axis_index("gy")
    n_x, n_y = lax.axis_size("gx"), lax.axis_size("gy")

    def inside(dx, dy):
        ok = None
        for place, step, count in ((gx, dx, n_x), (gy, dy, n_y)):
            if step == 0:
                continue
            here = (place + step < count) if step > 0 else (place + step >= 0)
            ok = here if ok is None else jnp.logical_and(ok, here)
        return ok

    def copy_of(key):
        way = key[2]
        index = keys.index(key)
        src, dst = out_buf[key], in_buf[key]
        if key[0] in ("raw", "source"):
            xs, ys = box(*key, dims_of[key[1]])
            src, dst = out_buf[key[:2] + WIDE[:1]].at[xs, ys], dst.at[xs, ys]
        return pltpu.make_async_remote_copy(
            src_ref=src,
            dst_ref=dst,
            send_sem=send_sem.at[index],
            recv_sem=recv_sem.at[index],
            device_id={"gx": gx + way[0], "gy": gy + way[1]},
            device_id_type=pl.DeviceIdType.MESH,
        )

    def send(group):
        for way in WIDE:
            chosen = [key for key in group if key[2] == way]
            if chosen:

                @pl.when(inside(*way))
                def _():
                    for key in chosen:
                        copy_of(key).start()

    def receive(group):
        for way in WIDE:
            chosen = [key for key in group if key[2] == way]
            if chosen:

                @pl.when(inside(-way[0], -way[1]))
                def _():
                    for key in chosen:
                        copy_of(key).wait_recv()

    def group_of(kind, level):
        return [key for key in keys if key[0] == kind and key[1] == level]

    stores = [pltpu.make_async_copy(kept[n], outs[n], store_sem.at[n]) for n in range(LEVELS)]
    loads = [pltpu.make_async_copy(args[n], held[n], load_sem.at[n]) for n in range(6)]

    barrier = pltpu.get_barrier_semaphore()
    for way in WIDE:

        @pl.when(inside(*way))
        def _():
            pl.semaphore_signal(
                barrier,
                inc=1,
                device_id={"gx": gx + way[0], "gy": gy + way[1]},
                device_id_type=pl.DeviceIdType.MESH,
            )

    for n in (0, 3, 4, 2, 5, 1):
        loads[n].start()

    def put_faces(kind, level, source, ways):
        for way in ways:
            xs, ys = at_side(dims_of[level], way)
            out_buf[(kind, level, way)][...] = source[xs, ys, :]

    size = pairs.shape[0]
    row = lax.broadcasted_iota(jnp.int32, (size, size // 2), 0)
    column = lax.broadcasted_iota(jnp.int32, (size, size // 2), 1)
    pairs[...] = jnp.where((row >> 1) == column, 1.0, 0.0).astype(jnp.bfloat16)
    for level in REACH:
        for name in WIDE_NAMES[:5]:
            wides[level][name][...] = jnp.zeros(wides[level][name].shape, jnp.float32)
    per[0]["shut"][...] = jnp.zeros(per[0]["shut"].shape, jnp.float32)

    loads[0].wait()
    put_faces("first", 0, u_in, FACES)

    def put_lower(level):
        for way, name in (((1, 0), "bx"), ((0, 1), "by")):
            xs, ys = at_side(dims_of[level], way)
            out_buf[("lower", level, way)][...] = per[level][name][xs, ys, :]

    loads[3].wait()
    per[0]["bx"][...] = bx_in[...].astype(jnp.float32)
    loads[4].wait()
    per[0]["by"][...] = by_in[...].astype(jnp.float32)
    put_lower(0)

    for way in AROUND:
        chosen = [key for key in keys if key[2] == way and key[0] not in ("raw", "source")]

        @pl.when(jnp.logical_not(inside(-way[0], -way[1])))
        def _():
            for key in chosen:
                in_buf[key][...] = jnp.zeros(in_buf[key].shape, jnp.float32)

    beside_x = (gx > 0).astype(jnp.int32) + (gx + 1 < n_x).astype(jnp.int32)
    beside_y = (gy > 0).astype(jnp.int32) + (gy + 1 < n_y).astype(jnp.int32)
    far_x = (gx > 1).astype(jnp.int32) + (gx + 2 < n_x).astype(jnp.int32)
    far_y = (gy > 1).astype(jnp.int32) + (gy + 2 < n_y).astype(jnp.int32)
    pl.semaphore_wait(barrier, beside_x + beside_y + beside_x * beside_y + far_x + far_y)

    send(group_of("lower", 0))
    send(group_of("first", 0))
    loads[2].wait()
    per[0]["a"][...] = a_in[...].astype(jnp.float32)
    loads[5].wait()
    per[0]["bz"][...] = bz_in[...].astype(jnp.float32)
    loads[1].wait()

    def three(v):
        high = v.astype(jnp.bfloat16)
        rest = v - high.astype(jnp.float32)
        mid = rest.astype(jnp.bfloat16)
        low = (rest - mid.astype(jnp.float32)).astype(jnp.bfloat16)
        return [high, mid, low]

    def sum_pairs_z(v):
        rows, size = v.shape
        parts = jnp.concatenate(three(v), axis=0)
        got = jnp.dot(parts, pairs[0:size, 0 : size // 2], preferred_element_type=jnp.float32)
        return got[:rows] + got[rows : 2 * rows] + got[2 * rows :]

    def squeeze(level, sources, ways):
        nx, ny, nz = dims_of[level]
        tmp, cols = pair_t[level], cols_t[level]
        hx, hy = nx // 2, ny // 2
        kept = len(sources)
        odd = (lax.broadcasted_iota(jnp.int32, (1, 1, nz), 2) & 1) == 1
        for n, (source, way) in enumerate(zip(sources, ways)):
            for i in range(hx):
                v = source(2 * i + 1)
                if way != 0:
                    v = source(2 * i) + v
                tmp[n * hx + i : n * hx + i + 1] = v
            some = slice(n * hx, (n + 1) * hx)
            for j in range(hy):
                v = tmp[some, 2 * j + 1 : 2 * j + 2, :]
                if way != 1:
                    v = v + tmp[some, 2 * j : 2 * j + 1, :]
                if way == 2:
                    v = jnp.where(odd, v, 0.0)
                cols[some, j : j + 1, :] = v * (0.125 if way is None else 0.25)
        total = kept * hx
        flat = cols[0:total].reshape(total * 8, nz)
        got = sum_pairs_z(flat).reshape(total, 8, nz // 2)
        return [got[n * hx : (n + 1) * hx, 0:hy, :] for n in range(kept)]

    def coarse_coefs(level):
        these = per[level]
        names = ("a", "bx", "by", "bz")
        sources = [
            functools.partial(lambda ref, i: ref[i : i + 1], these[name]) for name in names
        ]
        for name, v in zip(names, squeeze(level, sources, (None, 0, 1, 2))):
            per[level + 1][name][...] = v

    def make_coefs(level):
        these = per[level]
        nx, ny, nz = dims_of[level]
        scale = 0.25**level
        lower_x = in_buf[("lower", level, (1, 0))]
        lower_y = in_buf[("lower", level, (0, 1))]
        pad = these["open"]
        last = lax.broadcasted_iota(jnp.int32, (nx, ny, nz), 2)
        bx, by, bz = these["bx"][...], these["by"][...], these["bz"][...]
        bxl = jnp.concatenate([lower_x[...], bx[:-1]], axis=0) if nx > 1 else lower_x[...]
        pad[1 : 1 + nx, ROW : ROW + ny, :] = by
        pad[1 : 1 + nx, ROW - 1 : ROW, :] = lower_y[...]
        byl = pad[1 : 1 + nx, ROW - 1 : ROW - 1 + ny, :]
        bzl = jnp.where(last == 0, 0.0, pltpu.roll(bz, 1, 2))
        diag = these["a"][...] + scale * ((bx + bxl) + (by + byl) + (bz + bzl))
        over = 1.0 / diag
        these["diag"][...] = diag
        over_s = over * scale
        these["xu"][...] = bx * over_s
        these["xl"][...] = bxl * over_s
        these["yu"][...] = by * over_s
        these["yl"][...] = byl * over_s
        these["zu"][...] = jnp.where(last == nz - 1, 0.0, bz * over_s)
        these["zl"][...] = bzl * over_s
        return over

    toward_name = {(1, 0): "xu", (-1, 0): "xl", (0, 1): "yu", (0, -1): "yl"}

    def end_ways(way):
        return ((way[0], -1), (way[0], 1)) if way[0] else ((-1, way[1]), (1, way[1]))

    def cross(way, corner):
        return (0, corner[1]) if way[0] else (corner[0], 0)

    def put_toward(level):
        these = per[level]
        dims = dims_of[level]
        nx, ny, nz = dims
        for way in FACES:
            xs, ys = at_side(dims, way)
            shape = layer_shape(dims, way)
            offset = (xs.start + ys.start) & 1
            out_buf[("toward", level, way)][...] = jnp.where(
                parity_at(shape, offset), these[toward_name[way]][xs, ys, :], 0.0
            )
            for n, corner in enumerate(end_ways(way)):
                cxs, cys = at_side(dims, corner)
                offset = (cxs.start + cys.start) & 1
                out_buf[("ends", level, way)][n] = jnp.where(
                    parity_at((1, 1, nz), offset),
                    these[toward_name[cross(way, corner)]][cxs, cys, :],
                    0.0,
                )
        send(group_of("toward", level) + group_of("ends", level))

    def sums(level, pad):
        these = per[level]
        nx, ny, nz = dims_of[level]
        own = pad[1 : 1 + nx, ROW : ROW + ny, :]
        total = these["g"][...]
        total = total + these["xu"][...] * pad[2 : 2 + nx, ROW : ROW + ny, :]
        total = total + these["xl"][...] * pad[0:nx, ROW : ROW + ny, :]
        total = total + these["yu"][...] * pad[1 : 1 + nx, ROW + 1 : ROW + 1 + ny, :]
        total = total + these["yl"][...] * pad[1 : 1 + nx, ROW - 1 : ROW - 1 + ny, :]
        total = total + these["zu"][...] * pltpu.roll(own, nz - 1, 2)
        total = total + these["zl"][...] * pltpu.roll(own, 1, 2)
        return own, total

    def half_sweep(level, half, red):
        these = per[level]
        dims = dims_of[level]
        nx, ny, nz = dims
        shut, pad = these["shut"], these["open"]
        kind = "half%d" % half
        black = parity_at(dims)
        shut[1 : 1 + nx, ROW : ROW + ny, :] = red
        _, total = sums(level, shut)
        value = jnp.where(black, total, red)
        pad[1 : 1 + nx, ROW : ROW + ny, :] = value
        group = group_of(kind, level)
        for key in group:
            xs, ys = at_side(dims, key[2])
            out_buf[key][...] = pad[
                xs.start + 1 : xs.stop + 1, ys.start + ROW : ys.stop + ROW, :
            ]
        send(group)

    def finish_half(level, half, last):
        these = per[level]
        dims = dims_of[level]
        nx, ny, nz = dims
        pad = these["open"]
        kind = "half%d" % half
        group = group_of(kind, level)
        receive(group)
        if half == 0:
            receive(group_of("toward", level) + group_of("ends", level))
        back = lambda way: (-way[0], -way[1])
        if not last:
            for way in FACES:
                xs, ys = at_side(dims, way)
                mine = out_buf[(kind, level, way)][...]
                theirs = in_buf[(kind, level, back(way))][...]
                theirs = theirs + in_buf[("toward", level, back(way))][...] * mine
                hx, hy = halo_place(dims, way)
                pad[hx, hy, :] = theirs
                ends = in_buf[("ends", level, back(way))]
                for n, corner in enumerate(end_ways(way)):
                    cx, cy = at_side(dims, corner)
                    px = hx if way[0] else slice(1 + cx.start, 1 + cx.stop)
                    py = hy if way[1] else slice(ROW + cy.start, ROW + cy.stop)
                    column = in_buf[(kind, level, back(corner))][...]
                    pad[px, py, :] = pad[px, py, :] + ends[n] * column
        for way in FACES:
            xs, ys = at_side(dims, way)
            px = slice(1 + xs.start, 1 + xs.stop)
            py = slice(ROW + ys.start, ROW + ys.stop)
            theirs = in_buf[(kind, level, back(way))][...]
            pad[px, py, :] = pad[px, py, :] + out_buf[("toward", level, way)][...] * theirs

    def put_raw(level):
        buffer = out_buf[("raw", level, WIDE[0])]
        for c, name in enumerate(WIDE_NAMES[:4]):
            for y in range(dims_of[level][1]):
                buffer[:, y, c : c + 1, :] = per[level][name][:, y : y + 1, :]

    def spread(kind, level, ways, targets):
        nx, ny, _ = dims_of[level]
        reach = REACH[level]
        for way in ways:
            key = (kind, level, way)
            at_x, at_y = -nx * way[0], -ny * way[1]
            xs, ys = box(*key, dims_of[level])
            x_from, x_to = max(xs.start, -reach - at_x), min(xs.stop, nx + reach - at_x)
            y_from = max(ys.start, -reach - at_y)
            y_to = min(ys.stop, ny + reach - at_y)
            to = (at_y + y_from) % ROWS[level]
            planes = slice(at_x + x_from + reach, at_x + x_to + reach)

            @pl.when(inside(-way[0], -way[1]))
            def _():
                copy_of(key).wait_recv()
                if len(targets) == 1:
                    targets[0][planes, to : to + y_to - y_from, :] = in_buf[key][
                        x_from:x_to, y_from:y_to, :
                    ]
                else:
                    for c, target in enumerate(targets):
                        for y in range(y_from, y_to):
                            row = to + y - y_from
                            target[planes, row : row + 1, :] = in_buf[key][
                                x_from:x_to, y, c : c + 1, :
                            ]

    def lower_x(v):
        return jnp.concatenate([jnp.zeros_like(v[:1]), v[:-1]], axis=0)

    def wide_start(level):
        nx, ny, _ = dims_of[level]
        wide, reach = wides[level], REACH[level]
        for name in WIDE_NAMES[:4]:
            wide[name][reach : reach + nx, 0:ny, :] = per[level][name][...]

    def wide_diag(level, xs):
        wide = wides[level]
        scale = 0.25**level
        a, bx, by, bz = (wide[name][xs] for name in WIDE_NAMES[:4])
        place = lax.broadcasted_iota(jnp.int32, a.shape, 2)
        if xs.start > 0:
            bxl = wide["bx"][xs.start - 1 : xs.stop - 1]
        else:
            bxl = lower_x(bx)
        byl = pltpu.roll(by, 1, 1)
        bzl = jnp.where(place == 0, 0.0, pltpu.roll(bz, 1, 2))
        diag = a + scale * ((bx + bxl) + (by + byl) + (bz + bzl))
        over = jnp.where(a > 0.0, 1.0 / jnp.where(a > 0.0, diag, 1.0), 0.0)
        return diag, over, (bx, bxl, by, byl, bz, bzl)

    def wide_coefs(level):
        wide = wides[level]
        nz = dims_of[level][2]
        planes = wide["a"].shape[0]
        _, over, faces = wide_diag(level, slice(0, planes))
        over = over * 0.25**level
        bx, bxl, by, byl, bz, bzl = faces
        place = lax.broadcasted_iota(jnp.int32, bz.shape, 2)
        wide["xu"][...], wide["xl"][...] = bx * over, bxl * over
        wide["yu"][...], wide["yl"][...] = by * over, byl * over
        wide["zu"][...] = jnp.where(place == nz - 1, 0.0, bz * over)
        wide["zl"][...] = bzl * over

    def wide_sums(level, u, xs):
        wide = wides[level]
        nz, rows = dims_of[level][2], ROWS[level]
        own = u[1:-1]
        total = wide["g"][xs] + wide["xu"][xs] * u[2:] + wide["xl"][xs] * u[:-2]
        total = total + wide["yu"][xs] * pltpu.roll(own, rows - 1, 1)
        total = total + wide["yl"][xs] * pltpu.roll(own, 1, 1)
        total = total + wide["zu"][xs] * pltpu.roll(own, nz - 1, 2)
        total = total + wide["zl"][xs] * pltpu.roll(own, 1, 2)
        return own, total

    def wide_send(level, source):
        nx, ny, _ = dims_of[level]
        wide, reach = wides[level], REACH[level]
        own = source * wide["over"][reach : reach + nx, 0:ny, :]
        out_buf[("source", level, WIDE[0])][...] = own
        send(group_of("source", level))
        wide["g"][reach : reach + nx, 0:ny, :] = own

    def wide_smooth(level):
        nx, ny, _ = dims_of[level]
        reach = REACH[level]
        spread("source", level, WAYS[level], [wides[level]["g"]])
        g = wides[level]["g"][...]
        u = jnp.where(parity_at(g.shape, reach), 0.0, g)
        first = reach - 3
        if first == 0:
            edge = jnp.zeros_like(u[:1])
            u = jnp.concatenate([edge, u, edge], axis=0)
        for step in range(3):
            xs = slice(first, nx + 2 * reach - first)
            own, total = wide_sums(level, u, xs)
            black = parity_at(total.shape, reach + first)
            u = jnp.where(black, own, total) if step == 1 else jnp.where(black, total, own)
            first += 1
        return u

    dims = dims_of[0]
    nx, ny, nz = dims
    these = per[0]
    pad = these["open"]
    red_cells = jnp.logical_not(parity_at(dims))
    coarse_coefs(0)
    put_raw(1)
    send([key for key in group_of("raw", 1) if key[2] in FACES])
    wide_start(1)
    receive(group_of("lower", 0))
    these["g"][...] = f_in[...] * make_coefs(0)
    put_toward(0)
    receive(group_of("first", 0))
    pad[1 : 1 + nx, ROW : ROW + ny, :] = u_in[...]
    for way in FACES:
        hx, hy = halo_place(dims, way)
        pad[hx, hy, :] = in_buf[("first", 0, (-way[0], -way[1]))][...]
    own, total = sums(0, pad)
    half_sweep(0, 0, jnp.where(red_cells, total, own))
    send([key for key in group_of("raw", 1) if key[2] in CORNERS])
    coarse_coefs(1)
    put_raw(2)
    wide_start(2)
    finish_half(0, 0, False)
    own, total = sums(0, pad)
    half_sweep(0, 1, jnp.where(red_cells, total, own))
    send(group_of("raw", 2))
    spread("raw", 1, FACES, [wides[1][name] for name in WIDE_NAMES[:4]])
    middle = slice(REACH[1], REACH[1] + dims_of[1][0])
    diag, over, _ = wide_diag(1, middle)
    middle_diag = per[1]["bx"]
    middle_diag[...] = diag[:, 0 : dims_of[1][1], :]
    wides[1]["over"][middle] = over
    finish_half(0, 1, False)
    kept[0][...] = pad[1 : 1 + nx, ROW : ROW + ny, :]
    stores[0].start()
    own, total = sums(0, pad)
    these["a"][...] = jnp.where(red_cells, these["diag"][...] * (total - own), 0.0)
    take = functools.partial(lambda ref, i: ref[i : i + 1], these["a"])
    wide_send(1, squeeze(0, [take], (None,))[0])

    spread("raw", 1, CORNERS, [wides[1][name] for name in WIDE_NAMES[:4]])
    wide_coefs(1)
    spread("raw", 2, WAYS[2], [wides[2][name] for name in WIDE_NAMES[:4]])
    _, over, _ = wide_diag(2, slice(0, wides[2]["a"].shape[0]))
    wides[2]["over"][...] = over
    wide_coefs(2)
    u = wide_smooth(1)
    ny = dims_of[1][1]
    kept[1][...] = u[1:-1, 0:ny, :]
    stores[1].start()
    own, total = wide_sums(1, u, middle)
    red_cells = jnp.logical_not(parity_at(dims_of[1]))
    per[1]["a"][...] = jnp.where(
        red_cells, middle_diag[...] * (total[:, 0:ny, :] - own[:, 0:ny, :]), 0.0
    )
    take = functools.partial(lambda ref, i: ref[i : i + 1], per[1]["a"])
    wide_send(2, squeeze(1, [take], (None,))[0])

    def sent(chosen_of):
        for way in WIDE:
            chosen = [key for key in keys if key[2] == way and chosen_of(key)]

            @pl.when(inside(*way))
            def _():
                for key in chosen:
                    copy_of(key).wait_send()

    sent(lambda key: key[:2] != ("source", 2))
    u = wide_smooth(2)
    kept[2][...] = u[1:-1, 0 : dims_of[2][1], :]
    stores[2].start()
    sent(lambda key: key[:2] == ("source", 2))

    for copy in stores:
        copy.wait()


def store(*refs):
    given, outs, held, sem = refs[:3], refs[3:6], refs[6:9], refs[9]
    loads = [pltpu.make_async_copy(given[n], held[n], sem.at[n]) for n in range(3)]
    stores = [pltpu.make_async_copy(held[n], outs[n], sem.at[3 + n]) for n in range(3)]
    for copy in loads:
        copy.start()
    for load, copy in zip(loads, stores):
        load.wait()
        copy.start()
    for copy in stores:
        copy.wait()


def shards(solution, right_side, alpha, beta_x, beta_y, beta_z):
    dims_of = [tuple(size >> level for size in solution.shape) for level in range(LEVELS)]
    found = messages(dims_of)
    keys = list(found)
    buffers = [pltpu.VMEM(found[key], jnp.float32) for key in keys]
    fine = dims_of[0]
    scratch = [pltpu.VMEM(fine, jnp.float32)] * 2 + [pltpu.VMEM(fine, jnp.bfloat16)] * 4
    scratch += [pltpu.SemaphoreType.DMA((6,)), pltpu.SemaphoreType.DMA((LEVELS,))]
    scratch += [pltpu.VMEM(dims, jnp.float32) for dims in dims_of]
    scratch += buffers + buffers
    nx, ny, nz = fine
    scratch += [pltpu.VMEM((nx + 2, 24, nz), jnp.float32)] * 2
    scratch += [pltpu.VMEM(fine, jnp.float32)] * 12
    for level in REACH:
        scratch += [pltpu.VMEM(dims_of[level], jnp.float32)] * 4
    for nx, ny, nz in dims_of[:2]:
        scratch += [pltpu.VMEM((4 * nx // 2, ny, nz), jnp.float32)]
    for nx, ny, nz in dims_of[:2]:
        scratch += [pltpu.VMEM((4 * nx // 2, 8, nz), jnp.float32)]
    scratch += [pltpu.SemaphoreType.DMA((len(keys),))] * 2
    for level, reach in REACH.items():
        nx, _, nz = dims_of[level]
        scratch += [pltpu.VMEM((nx + 2 * reach, ROWS[level], nz), jnp.float32)] * 12
    scratch += [pltpu.VMEM((fine[2], fine[2] // 2), jnp.bfloat16)]
    iterates = pl.pallas_call(
        functools.partial(kernel, dims_of, keys),
        out_shape=[jax.ShapeDtypeStruct(dims, jnp.float32) for dims in dims_of],
        in_specs=[pl.BlockSpec(memory_space=pltpu.HBM)] * 6,
        out_specs=[pl.BlockSpec(memory_space=pltpu.HBM)] * 3,
        scratch_shapes=scratch,
        compiler_params=pltpu.CompilerParams(
            collective_id=0, has_side_effects=True, vmem_limit_bytes=VMEM_LIMIT
        ),
        name="vcycle",
    )(solution, right_side, alpha, beta_x, beta_y, beta_z)
    return pl.pallas_call(
        store,
        out_shape=[jax.ShapeDtypeStruct(dims, jnp.float32) for dims in dims_of],
        in_specs=[pl.BlockSpec(memory_space=pltpu.HBM)] * 3,
        out_specs=[pl.BlockSpec(memory_space=pltpu.HBM)] * 3,
        scratch_shapes=[pltpu.VMEM(dims, jnp.float32) for dims in dims_of]
        + [pltpu.SemaphoreType.DMA((6,))],
        compiler_params=pltpu.CompilerParams(vmem_limit_bytes=VMEM_LIMIT),
        name="store",
    )(*iterates)


def solution(mesh):
    place = P("gx", "gy", None)
    return jax.shard_map(
        shards,
        mesh=mesh,
        in_specs=(place,) * 6,
        out_specs=(place,) * 3,
        check_vma=False,
    )
```

```python
import functools

import jax
import jax.numpy as jnp
from jax import lax
from jax.experimental import pallas as pl
from jax.experimental.pallas import tpu as pltpu
from jax.sharding import PartitionSpec as P

LEVELS = 3
VMEM_LIMIT = (64 * 1024 - 160) * 1024
ROW = 8

FACES = ((0, 1), (0, -1), (1, 0), (-1, 0))
CORNERS = ((1, 1), (1, -1), (-1, 1), (-1, -1))
AROUND = FACES + CORNERS
FAR = ((2, 0), (-2, 0), (0, 2), (0, -2))
WIDE = AROUND + FAR
WIDE_NAMES = ("a", "bx", "by", "bz", "g", "over", "xu", "xl", "yu", "yl", "zu", "zl")
REACH = {1: 4, 2: 3}
ROWS = {1: 16, 2: 8}
WAYS = {1: AROUND, 2: WIDE}


def box(kind, level, way, dims):
    nx, ny, _ = dims
    if level == 2:
        return slice(0, nx), slice(0, ny)
    if kind == "source":
        xs = {0: (0, nx), 1: (1 if way[1] else 0, nx), -1: (0, 3 if way[1] else nx)}[way[0]]
        return slice(*xs), slice(0, ny)
    corner = way[0] != 0 and way[1] != 0
    least = {0: 0, 1: 1 if corner else 0, -1: 0}
    most = {0: 4, 1: 4, -1: 2 if way == (-1, -1) else 3}
    return slice(least[way[0]], most[way[0]]), slice(least[way[1]], most[way[1]])


def layer_shape(dims, way):
    nx, ny, nz = dims
    return (1 if way[0] else nx, 1 if way[1] else ny, nz)


def edge_shape(dims, way):
    return (2, 1, 1, dims[2])


def messages(dims_of):
    found = {}
    for way in FACES:
        found[("first", 0, way)] = layer_shape(dims_of[0], way)
    for level in REACH:
        nx, ny, nz = dims_of[level]
        for way in WAYS[level]:
            found[("raw", level, way)] = (nx, ny, 4, nz)
            found[("source", level, way)] = (nx, ny, nz)
    dims = dims_of[0]
    for way in ((1, 0), (0, 1)):
        found[("lower", 0, way)] = layer_shape(dims, way)
    for way in FACES:
        found[("toward", 0, way)] = layer_shape(dims, way)
        found[("ends", 0, way)] = edge_shape(dims, way)
    for half in range(2):
        for way in AROUND:
            found[("half%d" % half, 0, way)] = layer_shape(dims, way)
    return found


def at_side(dims, way):
    nx, ny, _ = dims
    xs = {0: slice(0, nx), 1: slice(nx - 1, nx), -1: slice(0, 1)}[way[0]]
    ys = {0: slice(0, ny), 1: slice(ny - 1, ny), -1: slice(0, 1)}[way[1]]
    return xs, ys


def halo_place(dims, way):
    nx, ny, _ = dims
    xs = {0: slice(1, 1 + nx), 1: slice(nx + 1, nx + 2), -1: slice(0, 1)}[way[0]]
    ys = {0: slice(ROW, ROW + ny), 1: slice(ROW + ny, ROW + ny + 1), -1: slice(ROW - 1, ROW)}[way[1]]
    return xs, ys


def parity_at(shape, offset=0):
    total = (
        lax.broadcasted_iota(jnp.int32, shape, 0)
        + lax.broadcasted_iota(jnp.int32, shape, 1)
        + lax.broadcasted_iota(jnp.int32, shape, 2)
        + offset
    )
    return (total & 1) == 1


def kernel(dims_of, keys, *refs):
    refs = list(refs)
    args = refs[:6]
    outs = refs[6:9]
    u_in, f_in, a_in, bx_in, by_in, bz_in = held = refs[9:15]
    load_sem, store_sem = refs[15:17]
    kept = refs[17:20]
    refs = refs[20:]
    n_keys = len(keys)
    out_buf = dict(zip(keys, refs[:n_keys]))
    in_buf = dict(zip(keys, refs[n_keys : 2 * n_keys]))
    refs = refs[2 * n_keys :]
    names = ("open", "shut", "g", "diag", "xu", "xl", "yu", "yl", "zu", "zl", "a", "bx", "by", "bz")
    per = [dict(zip(names, refs[:14]))]
    refs = refs[14:]
    for level in REACH:
        per.append(dict(zip(names[-4:], refs[:4])))
        refs = refs[4:]
    pair_t, cols_t = refs[0:2], refs[2:4]
    send_sem, recv_sem = refs[4], refs[5]
    wides = {1: dict(zip(WIDE_NAMES, refs[6:18])), 2: dict(zip(WIDE_NAMES, refs[18:30]))}
    pairs = refs[30]

    gx, gy = lax.axis_index("gx"), lax.axis_index("gy")
    n_x, n_y = lax.axis_size("gx"), lax.axis_size("gy")

    def inside(dx, dy):
        ok = None
        for place, step, count in ((gx, dx, n_x), (gy, dy, n_y)):
            if step == 0:
                continue
            here = (place + step < count) if step > 0 else (place + step >= 0)
            ok = here if ok is None else jnp.logical_and(ok, here)
        return ok

    def copy_of(key):
        way = key[2]
        index = keys.index(key)
        src, dst = out_buf[key], in_buf[key]
        if key[0] in ("raw", "source"):
            xs, ys = box(*key, dims_of[key[1]])
            src, dst = out_buf[key[:2] + WIDE[:1]].at[xs, ys], dst.at[xs, ys]
        return pltpu.make_async_remote_copy(
            src_ref=src,
            dst_ref=dst,
            send_sem=send_sem.at[index],
            recv_sem=recv_sem.at[index],
            device_id={"gx": gx + way[0], "gy": gy + way[1]},
            device_id_type=pl.DeviceIdType.MESH,
        )

    def send(group):
        for way in WIDE:
            chosen = [key for key in group if key[2] == way]
            if chosen:

                @pl.when(inside(*way))
                def _():
                    for key in chosen:
                        copy_of(key).start()

    def receive(group):
        for way in WIDE:
            chosen = [key for key in group if key[2] == way]
            if chosen:

                @pl.when(inside(-way[0], -way[1]))
                def _():
                    for key in chosen:
                        copy_of(key).wait_recv()

    def group_of(kind, level):
        return [key for key in keys if key[0] == kind and key[1] == level]

    stores = [pltpu.make_async_copy(kept[n], outs[n], store_sem.at[n]) for n in range(LEVELS)]
    loads = [pltpu.make_async_copy(args[n], held[n], load_sem.at[n]) for n in range(6)]

    barrier = pltpu.get_barrier_semaphore()
    for way in WIDE:

        @pl.when(inside(*way))
        def _():
            pl.semaphore_signal(
                barrier,
                inc=1,
                device_id={"gx": gx + way[0], "gy": gy + way[1]},
                device_id_type=pl.DeviceIdType.MESH,
            )

    for n in (0, 3, 4, 2, 5, 1):
        loads[n].start()

    def put_faces(kind, level, source, ways):
        for way in ways:
            xs, ys = at_side(dims_of[level], way)
            out_buf[(kind, level, way)][...] = source[xs, ys, :]

    size = pairs.shape[0]
    row = lax.broadcasted_iota(jnp.int32, (size, size // 2), 0)
    column = lax.broadcasted_iota(jnp.int32, (size, size // 2), 1)
    pairs[...] = jnp.where((row >> 1) == column, 1.0, 0.0).astype(jnp.bfloat16)
    for level in REACH:
        for name in WIDE_NAMES[:5]:
            wides[level][name][...] = jnp.zeros(wides[level][name].shape, jnp.float32)
    per[0]["shut"][...] = jnp.zeros(per[0]["shut"].shape, jnp.float32)

    loads[0].wait()
    put_faces("first", 0, u_in, FACES)

    def put_lower(level):
        for way, name in (((1, 0), "bx"), ((0, 1), "by")):
            xs, ys = at_side(dims_of[level], way)
            out_buf[("lower", level, way)][...] = per[level][name][xs, ys, :]

    loads[3].wait()
    per[0]["bx"][...] = bx_in[...].astype(jnp.float32)
    loads[4].wait()
    per[0]["by"][...] = by_in[...].astype(jnp.float32)
    put_lower(0)

    for way in AROUND:
        chosen = [key for key in keys if key[2] == way and key[0] not in ("raw", "source")]

        @pl.when(jnp.logical_not(inside(-way[0], -way[1])))
        def _():
            for key in chosen:
                in_buf[key][...] = jnp.zeros(in_buf[key].shape, jnp.float32)

    beside_x = (gx > 0).astype(jnp.int32) + (gx + 1 < n_x).astype(jnp.int32)
    beside_y = (gy > 0).astype(jnp.int32) + (gy + 1 < n_y).astype(jnp.int32)
    far_x = (gx > 1).astype(jnp.int32) + (gx + 2 < n_x).astype(jnp.int32)
    far_y = (gy > 1).astype(jnp.int32) + (gy + 2 < n_y).astype(jnp.int32)
    pl.semaphore_wait(barrier, beside_x + beside_y + beside_x * beside_y + far_x + far_y)

    send(group_of("lower", 0))
    send(group_of("first", 0))
    loads[2].wait()
    per[0]["a"][...] = a_in[...].astype(jnp.float32)
    loads[5].wait()
    per[0]["bz"][...] = bz_in[...].astype(jnp.float32)
    loads[1].wait()

    def three(v):
        high = v.astype(jnp.bfloat16)
        rest = v - high.astype(jnp.float32)
        mid = rest.astype(jnp.bfloat16)
        low = (rest - mid.astype(jnp.float32)).astype(jnp.bfloat16)
        return [high, mid, low]

    def sum_pairs_z(v):
        rows, size = v.shape
        parts = jnp.concatenate(three(v), axis=0)
        got = jnp.dot(parts, pairs[0:size, 0 : size // 2], preferred_element_type=jnp.float32)
        return got[:rows] + got[rows : 2 * rows] + got[2 * rows :]

    def squeeze(level, sources, ways):
        nx, ny, nz = dims_of[level]
        tmp, cols = pair_t[level], cols_t[level]
        hx, hy = nx // 2, ny // 2
        kept = len(sources)
        odd = (lax.broadcasted_iota(jnp.int32, (1, 1, nz), 2) & 1) == 1
        for n, (source, way) in enumerate(zip(sources, ways)):
            for i in range(hx):
                v = source(2 * i + 1)
                if way != 0:
                    v = source(2 * i) + v
                tmp[n * hx + i : n * hx + i + 1] = v
            some = slice(n * hx, (n + 1) * hx)
            for j in range(hy):
                v = tmp[some, 2 * j + 1 : 2 * j + 2, :]
                if way != 1:
                    v = v + tmp[some, 2 * j : 2 * j + 1, :]
                if way == 2:
                    v = jnp.where(odd, v, 0.0)
                cols[some, j : j + 1, :] = v * (0.125 if way is None else 0.25)
        total = kept * hx
        flat = cols[0:total].reshape(total * 8, nz)
        got = sum_pairs_z(flat).reshape(total, 8, nz // 2)
        return [got[n * hx : (n + 1) * hx, 0:hy, :] for n in range(kept)]

    def coarse_coefs(level):
        these = per[level]
        names = ("a", "bx", "by", "bz")
        sources = [
            functools.partial(lambda ref, i: ref[i : i + 1], these[name]) for name in names
        ]
        for name, v in zip(names, squeeze(level, sources, (None, 0, 1, 2))):
            per[level + 1][name][...] = v

    def make_coefs(level):
        these = per[level]
        nx, ny, nz = dims_of[level]
        scale = 0.25**level
        lower_x = in_buf[("lower", level, (1, 0))]
        lower_y = in_buf[("lower", level, (0, 1))]
        pad = these["open"]
        last = lax.broadcasted_iota(jnp.int32, (nx, ny, nz), 2)
        bx, by, bz = these["bx"][...], these["by"][...], these["bz"][...]
        bxl = jnp.concatenate([lower_x[...], bx[:-1]], axis=0) if nx > 1 else lower_x[...]
        pad[1 : 1 + nx, ROW : ROW + ny, :] = by
        pad[1 : 1 + nx, ROW - 1 : ROW, :] = lower_y[...]
        byl = pad[1 : 1 + nx, ROW - 1 : ROW - 1 + ny, :]
        bzl = jnp.where(last == 0, 0.0, pltpu.roll(bz, 1, 2))
        diag = these["a"][...] + scale * ((bx + bxl) + (by + byl) + (bz + bzl))
        over = 1.0 / diag
        these["diag"][...] = diag
        over_s = over * scale
        these["xu"][...] = bx * over_s
        these["xl"][...] = bxl * over_s
        these["yu"][...] = by * over_s
        these["yl"][...] = byl * over_s
        these["zu"][...] = jnp.where(last == nz - 1, 0.0, bz * over_s)
        these["zl"][...] = bzl * over_s
        return over

    toward_name = {(1, 0): "xu", (-1, 0): "xl", (0, 1): "yu", (0, -1): "yl"}

    def end_ways(way):
        return ((way[0], -1), (way[0], 1)) if way[0] else ((-1, way[1]), (1, way[1]))

    def cross(way, corner):
        return (0, corner[1]) if way[0] else (corner[0], 0)

    def put_toward(level):
        these = per[level]
        dims = dims_of[level]
        nx, ny, nz = dims
        for way in FACES:
            xs, ys = at_side(dims, way)
            shape = layer_shape(dims, way)
            offset = (xs.start + ys.start) & 1
            out_buf[("toward", level, way)][...] = jnp.where(
                parity_at(shape, offset), these[toward_name[way]][xs, ys, :], 0.0
            )
            for n, corner in enumerate(end_ways(way)):
                cxs, cys = at_side(dims, corner)
                offset = (cxs.start + cys.start) & 1
                out_buf[("ends", level, way)][n] = jnp.where(
                    parity_at((1, 1, nz), offset),
                    these[toward_name[cross(way, corner)]][cxs, cys, :],
                    0.0,
                )
        send(group_of("toward", level) + group_of("ends", level))

    def planes(pad, write):
        these = per[0]
        nx, ny, nz = dims_of[0]
        rows, below, above = (slice(ROW + n, ROW + n + ny) for n in (0, -1, 1))

        def step(x, carry):
            here, low, high = pl.ds(x, 1), pl.ds(x + 1, 1), pl.ds(x + 2, 1)
            own = pad[low, rows, :]
            total = these["g"][here] + these["xu"][here] * pad[high, rows, :]
            total = total + these["xl"][here] * pad[here, rows, :]
            total = total + these["yu"][here] * pad[low, above, :]
            total = total + these["yl"][here] * pad[low, below, :]
            total = total + these["zu"][here] * pltpu.roll(own, nz - 1, 2)
            total = total + these["zl"][here] * pltpu.roll(own, 1, 2)
            write(x, own, total, jnp.logical_not(parity_at((1, ny, nz), x)))
            return carry

        lax.fori_loop(0, nx, step, 0, unroll=2)

    def colour_step(source, target, colour):
        def write(x, own, total, red):
            new = jnp.where(red, total, own) if colour == 0 else jnp.where(red, own, total)
            target[pl.ds(x + 1, 1), ROW : ROW + dims_of[0][1], :] = new

        planes(source, write)

    def half_sweep(level, half):
        these = per[level]
        dims = dims_of[level]
        nx, ny, nz = dims
        shut, pad = these["shut"], these["open"]
        kind = "half%d" % half
        colour_step(pad, shut, 0)
        colour_step(shut, pad, 1)
        group = group_of(kind, level)
        for key in group:
            xs, ys = at_side(dims, key[2])
            out_buf[key][...] = pad[
                xs.start + 1 : xs.stop + 1, ys.start + ROW : ys.stop + ROW, :
            ]
        send(group)

    def finish_half(level, half, last):
        these = per[level]
        dims = dims_of[level]
        nx, ny, nz = dims
        pad = these["open"]
        kind = "half%d" % half
        group = group_of(kind, level)
        receive(group)
        if half == 0:
            receive(group_of("toward", level) + group_of("ends", level))
        back = lambda way: (-way[0], -way[1])
        if not last:
            for way in FACES:
                xs, ys = at_side(dims, way)
                mine = out_buf[(kind, level, way)][...]
                theirs = in_buf[(kind, level, back(way))][...]
                theirs = theirs + in_buf[("toward", level, back(way))][...] * mine
                hx, hy = halo_place(dims, way)
                pad[hx, hy, :] = theirs
                ends = in_buf[("ends", level, back(way))]
                for n, corner in enumerate(end_ways(way)):
                    cx, cy = at_side(dims, corner)
                    px = hx if way[0] else slice(1 + cx.start, 1 + cx.stop)
                    py = hy if way[1] else slice(ROW + cy.start, ROW + cy.stop)
                    column = in_buf[(kind, level, back(corner))][...]
                    pad[px, py, :] = pad[px, py, :] + ends[n] * column
        for way in FACES:
            xs, ys = at_side(dims, way)
            px = slice(1 + xs.start, 1 + xs.stop)
            py = slice(ROW + ys.start, ROW + ys.stop)
            theirs = in_buf[(kind, level, back(way))][...]
            pad[px, py, :] = pad[px, py, :] + out_buf[("toward", level, way)][...] * theirs

    def put_raw(level):
        buffer = out_buf[("raw", level, WIDE[0])]
        for c, name in enumerate(WIDE_NAMES[:4]):
            for y in range(dims_of[level][1]):
                buffer[:, y, c : c + 1, :] = per[level][name][:, y : y + 1, :]

    def spread(kind, level, ways, targets):
        nx, ny, _ = dims_of[level]
        reach = REACH[level]
        for way in ways:
            key = (kind, level, way)
            at_x, at_y = -nx * way[0], -ny * way[1]
            xs, ys = box(*key, dims_of[level])
            x_from, x_to = max(xs.start, -reach - at_x), min(xs.stop, nx + reach - at_x)
            y_from = max(ys.start, -reach - at_y)
            y_to = min(ys.stop, ny + reach - at_y)
            to = (at_y + y_from) % ROWS[level]
            planes = slice(at_x + x_from + reach, at_x + x_to + reach)

            @pl.when(inside(-way[0], -way[1]))
            def _():
                copy_of(key).wait_recv()
                if len(targets) == 1:
                    targets[0][planes, to : to + y_to - y_from, :] = in_buf[key][
                        x_from:x_to, y_from:y_to, :
                    ]
                else:
                    for c, target in enumerate(targets):
                        for y in range(y_from, y_to):
                            row = to + y - y_from
                            target[planes, row : row + 1, :] = in_buf[key][
                                x_from:x_to, y, c : c + 1, :
                            ]

    def lower_x(v):
        return jnp.concatenate([jnp.zeros_like(v[:1]), v[:-1]], axis=0)

    def wide_start(level):
        nx, ny, _ = dims_of[level]
        wide, reach = wides[level], REACH[level]
        for name in WIDE_NAMES[:4]:
            wide[name][reach : reach + nx, 0:ny, :] = per[level][name][...]

    def wide_diag(level, xs):
        wide = wides[level]
        scale = 0.25**level
        a, bx, by, bz = (wide[name][xs] for name in WIDE_NAMES[:4])
        place = lax.broadcasted_iota(jnp.int32, a.shape, 2)
        if xs.start > 0:
            bxl = wide["bx"][xs.start - 1 : xs.stop - 1]
        else:
            bxl = lower_x(bx)
        byl = pltpu.roll(by, 1, 1)
        bzl = jnp.where(place == 0, 0.0, pltpu.roll(bz, 1, 2))
        diag = a + scale * ((bx + bxl) + (by + byl) + (bz + bzl))
        over = jnp.where(a > 0.0, 1.0 / jnp.where(a > 0.0, diag, 1.0), 0.0)
        return diag, over, (bx, bxl, by, byl, bz, bzl)

    def wide_coefs(level):
        wide = wides[level]
        nz = dims_of[level][2]
        planes = wide["a"].shape[0]
        _, over, faces = wide_diag(level, slice(0, planes))
        over = over * 0.25**level
        bx, bxl, by, byl, bz, bzl = faces
        place = lax.broadcasted_iota(jnp.int32, bz.shape, 2)
        wide["xu"][...], wide["xl"][...] = bx * over, bxl * over
        wide["yu"][...], wide["yl"][...] = by * over, byl * over
        wide["zu"][...] = jnp.where(place == nz - 1, 0.0, bz * over)
        wide["zl"][...] = bzl * over

    def wide_sums(level, u, xs):
        wide = wides[level]
        nz, rows = dims_of[level][2], ROWS[level]
        own = u[1:-1]
        total = wide["g"][xs] + wide["xu"][xs] * u[2:] + wide["xl"][xs] * u[:-2]
        total = total + wide["yu"][xs] * pltpu.roll(own, rows - 1, 1)
        total = total + wide["yl"][xs] * pltpu.roll(own, 1, 1)
        total = total + wide["zu"][xs] * pltpu.roll(own, nz - 1, 2)
        total = total + wide["zl"][xs] * pltpu.roll(own, 1, 2)
        return own, total

    def wide_send(level, source):
        nx, ny, _ = dims_of[level]
        wide, reach = wides[level], REACH[level]
        own = source * wide["over"][reach : reach + nx, 0:ny, :]
        out_buf[("source", level, WIDE[0])][...] = own
        send(group_of("source", level))
        wide["g"][reach : reach + nx, 0:ny, :] = own

    def wide_smooth(level):
        nx, ny, _ = dims_of[level]
        reach = REACH[level]
        spread("source", level, WAYS[level], [wides[level]["g"]])
        g = wides[level]["g"][...]
        u = jnp.where(parity_at(g.shape, reach), 0.0, g)
        first = reach - 3
        if first == 0:
            edge = jnp.zeros_like(u[:1])
            u = jnp.concatenate([edge, u, edge], axis=0)
        for step in range(3):
            xs = slice(first, nx + 2 * reach - first)
            own, total = wide_sums(level, u, xs)
            black = parity_at(total.shape, reach + first)
            u = jnp.where(black, own, total) if step == 1 else jnp.where(black, total, own)
            first += 1
        return u

    dims = dims_of[0]
    nx, ny, nz = dims
    these = per[0]
    pad = these["open"]
    coarse_coefs(0)
    put_raw(1)
    send([key for key in group_of("raw", 1) if key[2] in FACES])
    wide_start(1)
    receive(group_of("lower", 0))
    these["g"][...] = f_in[...] * make_coefs(0)
    put_toward(0)
    receive(group_of("first", 0))
    pad[1 : 1 + nx, ROW : ROW + ny, :] = u_in[...]
    for way in FACES:
        hx, hy = halo_place(dims, way)
        pad[hx, hy, :] = in_buf[("first", 0, (-way[0], -way[1]))][...]
    half_sweep(0, 0)
    send([key for key in group_of("raw", 1) if key[2] in CORNERS])
    coarse_coefs(1)
    put_raw(2)
    wide_start(2)
    finish_half(0, 0, False)
    half_sweep(0, 1)
    send(group_of("raw", 2))
    spread("raw", 1, FACES, [wides[1][name] for name in WIDE_NAMES[:4]])
    middle = slice(REACH[1], REACH[1] + dims_of[1][0])
    diag, over, _ = wide_diag(1, middle)
    middle_diag = per[1]["bx"]
    middle_diag[...] = diag[:, 0 : dims_of[1][1], :]
    wides[1]["over"][middle] = over
    finish_half(0, 1, False)
    kept[0][...] = pad[1 : 1 + nx, ROW : ROW + ny, :]
    stores[0].start()

    def write(x, own, total, red):
        here = pl.ds(x, 1)
        these["a"][here] = jnp.where(red, these["diag"][here] * (total - own), 0.0)

    planes(pad, write)
    take = functools.partial(lambda ref, i: ref[i : i + 1], these["a"])
    wide_send(1, squeeze(0, [take], (None,))[0])

    spread("raw", 1, CORNERS, [wides[1][name] for name in WIDE_NAMES[:4]])
    wide_coefs(1)
    spread("raw", 2, WAYS[2], [wides[2][name] for name in WIDE_NAMES[:4]])
    _, over, _ = wide_diag(2, slice(0, wides[2]["a"].shape[0]))
    wides[2]["over"][...] = over
    wide_coefs(2)
    u = wide_smooth(1)
    ny = dims_of[1][1]
    kept[1][...] = u[1:-1, 0:ny, :]
    stores[1].start()
    own, total = wide_sums(1, u, middle)
    red_cells = jnp.logical_not(parity_at(dims_of[1]))
    per[1]["a"][...] = jnp.where(
        red_cells, middle_diag[...] * (total[:, 0:ny, :] - own[:, 0:ny, :]), 0.0
    )
    take = functools.partial(lambda ref, i: ref[i : i + 1], per[1]["a"])
    wide_send(2, squeeze(1, [take], (None,))[0])

    def sent(chosen_of):
        for way in WIDE:
            chosen = [key for key in keys if key[2] == way and chosen_of(key)]

            @pl.when(inside(*way))
            def _():
                for key in chosen:
                    copy_of(key).wait_send()

    sent(lambda key: key[:2] != ("source", 2))
    u = wide_smooth(2)
    kept[2][...] = u[1:-1, 0 : dims_of[2][1], :]
    stores[2].start()
    sent(lambda key: key[:2] == ("source", 2))

    for copy in stores:
        copy.wait()


def store(*refs):
    given, outs, held, sem = refs[:3], refs[3:6], refs[6:9], refs[9]
    loads = [pltpu.make_async_copy(given[n], held[n], sem.at[n]) for n in range(3)]
    stores = [pltpu.make_async_copy(held[n], outs[n], sem.at[3 + n]) for n in range(3)]
    for copy in loads:
        copy.start()
    for load, copy in zip(loads, stores):
        load.wait()
        copy.start()
    for copy in stores:
        copy.wait()


def shards(solution, right_side, alpha, beta_x, beta_y, beta_z):
    dims_of = [tuple(size >> level for size in solution.shape) for level in range(LEVELS)]
    found = messages(dims_of)
    keys = list(found)
    buffers = [pltpu.VMEM(found[key], jnp.float32) for key in keys]
    fine = dims_of[0]
    scratch = [pltpu.VMEM(fine, jnp.float32)] * 2 + [pltpu.VMEM(fine, jnp.bfloat16)] * 4
    scratch += [pltpu.SemaphoreType.DMA((6,)), pltpu.SemaphoreType.DMA((LEVELS,))]
    scratch += [pltpu.VMEM(dims, jnp.float32) for dims in dims_of]
    scratch += buffers + buffers
    nx, ny, nz = fine
    scratch += [pltpu.VMEM((nx + 2, 24, nz), jnp.float32)] * 2
    scratch += [pltpu.VMEM(fine, jnp.float32)] * 12
    for level in REACH:
        scratch += [pltpu.VMEM(dims_of[level], jnp.float32)] * 4
    for nx, ny, nz in dims_of[:2]:
        scratch += [pltpu.VMEM((4 * nx // 2, ny, nz), jnp.float32)]
    for nx, ny, nz in dims_of[:2]:
        scratch += [pltpu.VMEM((4 * nx // 2, 8, nz), jnp.float32)]
    scratch += [pltpu.SemaphoreType.DMA((len(keys),))] * 2
    for level, reach in REACH.items():
        nx, _, nz = dims_of[level]
        scratch += [pltpu.VMEM((nx + 2 * reach, ROWS[level], nz), jnp.float32)] * 12
    scratch += [pltpu.VMEM((fine[2], fine[2] // 2), jnp.bfloat16)]
    iterates = pl.pallas_call(
        functools.partial(kernel, dims_of, keys),
        out_shape=[jax.ShapeDtypeStruct(dims, jnp.float32) for dims in dims_of],
        in_specs=[pl.BlockSpec(memory_space=pltpu.HBM)] * 6,
        out_specs=[pl.BlockSpec(memory_space=pltpu.HBM)] * 3,
        scratch_shapes=scratch,
        compiler_params=pltpu.CompilerParams(
            collective_id=0, has_side_effects=True, vmem_limit_bytes=VMEM_LIMIT
        ),
        name="vcycle",
    )(solution, right_side, alpha, beta_x, beta_y, beta_z)
    return pl.pallas_call(
        store,
        out_shape=[jax.ShapeDtypeStruct(dims, jnp.float32) for dims in dims_of],
        in_specs=[pl.BlockSpec(memory_space=pltpu.HBM)] * 3,
        out_specs=[pl.BlockSpec(memory_space=pltpu.HBM)] * 3,
        scratch_shapes=[pltpu.VMEM(dims, jnp.float32) for dims in dims_of]
        + [pltpu.SemaphoreType.DMA((6,))],
        compiler_params=pltpu.CompilerParams(vmem_limit_bytes=VMEM_LIMIT),
        name="store",
    )(*iterates)


def solution(mesh):
    place = P("gx", "gy", None)
    return jax.shard_map(
        shards,
        mesh=mesh,
        in_specs=(place,) * 6,
        out_specs=(place,) * 3,
        check_vma=False,
    )
```
